128 devices in a mesh: dp: 8 (over x, core), mp: 16 (over y, z).
Axes of the slice: x: 4, y: 4, z: 4, core: 2. Of those that a mesh axis runs over, the one named last changes fastest.
Arguments:
- tokens: bfloat16 [512, 8192], P('dp', 'mp'), may hold values from -80 to 80
- frozen_gate_weight: bfloat16 [8192, 28672], P('mp', 'dp'), may hold values from -0.198873782 to 0.198873782
- frozen_up_weight: bfloat16 [8192, 28672], P('mp', 'dp'), may hold values from -0.198873782 to 0.198873782
- frozen_down_weight: bfloat16 [28672, 8192], P('dp', 'mp'), may hold values from -0.28347335 to 0.28347335
- gate_left_factor: bfloat16 [8192, 16], P('mp'), may hold values from -0.0625 to 0.0625
- gate_right_factor: bfloat16 [16, 28672], P(None, 'dp'), may hold values from -0.75 to 0.75
- up_left_factor: bfloat16 [8192, 16], P('mp'), may hold values from -0.0625 to 0.0625
- up_right_factor: bfloat16 [16, 28672], P(None, 'dp'), may hold values from -0.75 to 0.75
- down_left_factor: bfloat16 [28672, 16], P('dp'), may hold values from -0.03125 to 0.03125
- down_right_factor: bfloat16 [16, 8192], P(None, 'mp'), may hold values from -0.75 to 0.75
- gate_column_magnitude: float32 [28672], P('dp'), may hold values from 0.5 to 2
- up_column_magnitude: float32 [28672], P('dp'), may hold values from 0.5 to 2
- down_column_magnitude: float32 [8192], P('mp'), may hold values from 0.5 to 2
- cotangent: bfloat16 [512, 8192], P('dp', 'mp'), may hold values from -80 to 80
Outputs:
- feedforward_output: bfloat16 [512, 8192], P('dp', 'mp')
- token_input_gradient: bfloat16 [512, 8192], P('dp', 'mp')
- gate_magnitude_gradient: float32 [28672], P('dp')
- up_magnitude_gradient: float32 [28672], P('dp')
- down_magnitude_gradient: float32 [8192], P('mp')
- gate_right_factor_gradient: float32 [16, 28672], P(None, 'dp')
- gate_left_factor_gradient: float32 [8192, 16], P('mp')
- up_right_factor_gradient: float32 [16, 28672], P(None, 'dp')
- up_left_factor_gradient: float32 [8192, 16], P('mp')
- down_right_factor_gradient: float32 [16, 8192], P(None, 'mp')
- down_left_factor_gradient: float32 [28672, 16], P('dp')
The draws below stay inside these ranges and needn't reach their ends.
All inputs are finite; a program needn't handle non-finite values.
Results may differ from the reference program's by a relative error of at most 0.03.
Values may be sent and summed in bfloat16 or wider, within the bound.
A program may use at most 192 MiB of HBM per device.

```python
import math
import jax
import jax.numpy as jnp
from jax import lax

MODEL_WIDTH = 8192
HIDDEN_UNITS = 28672
ADAPTER_RANK = 16
TOKENS = 512
N_MP = 16


def scaled_rows(key, num_rows, num_cols, base, salt, steep):
    noise_key, scale_key, column_key = jax.random.split(jax.random.fold_in(key, salt), 3)
    noise = jnp.clip(jax.random.normal(noise_key, (num_rows, num_cols), jnp.float32), -4.0, 4.0)
    spread = 0.5756463
    position = jnp.arange(num_rows, dtype=jnp.float32) / max(num_rows - 1, 1)
    if steep > 0:
        rising = jnp.exp(2.0794415 * (position - 0.5))
    elif steep < 0:
        rising = jnp.exp(-2.0794415 * (position - 0.5))
    else:
        rising = jnp.sqrt((1.0 + 2.0 * position) / 2.0)
    jitter = jnp.exp(jax.random.uniform(scale_key, (num_rows,), jnp.float32, -spread, spread))
    column_scale = jnp.exp(jax.random.uniform(column_key, (num_cols,), jnp.float32, -0.7, 0.7))
    return noise * (rising * jitter * base)[:, None] * column_scale[None, :]


def draw_tokens(key, part):
    return scaled_rows(key, TOKENS, MODEL_WIDTH, 1.0, 101, 1).astype(jnp.bfloat16)


def draw_cotangent(key, part):
    return scaled_rows(key, TOKENS, MODEL_WIDTH, 1.0, 202, -1).astype(jnp.bfloat16)


def draw_frozen_gate_weight(key, part):
    return scaled_rows(key, MODEL_WIDTH, HIDDEN_UNITS, MODEL_WIDTH ** (-0.5), 303, 0).astype(jnp.bfloat16)


def draw_frozen_up_weight(key, part):
    return scaled_rows(key, MODEL_WIDTH, HIDDEN_UNITS, MODEL_WIDTH ** (-0.5), 404, 0).astype(jnp.bfloat16)


def draw_frozen_down_weight(key, part):
    return scaled_rows(key, HIDDEN_UNITS, MODEL_WIDTH, HIDDEN_UNITS ** (-0.5), 505, 1).astype(jnp.bfloat16)


def block_levels(stream_key, dims, cuts, smallest, top_value):
    loudness = 1.0
    for axis_at, parts in cuts:
        heights = jax.random.uniform(jax.random.fold_in(jax.random.fold_in(stream_key, 6), axis_at), (parts,), jnp.float32, smallest / len(cuts), top_value / len(cuts))
        loudness = loudness * jnp.repeat(jnp.exp(heights), dims[axis_at] // parts).reshape((-1,) + (1,) * (len(dims) - 1 - axis_at))
    return loudness


def normal_values(rng, shape, deviation, most, pieces=(), kind=jnp.bfloat16):
    gain = block_levels(rng, shape, pieces, -0.22, 0.18) if pieces else 1.0
    drawn = jax.random.normal(rng, shape, jnp.float32) * deviation * gain
    return jnp.minimum(jnp.maximum(drawn, -most), most).astype(kind)


def setup_inputs(seed: int = 0) -> dict:
    splits = jax.random.split(jax.random.key(seed), 15)
    tokens = draw_tokens(jax.random.fold_in(splits[14], 71), 0)
    frozen_gate_weight = draw_frozen_gate_weight(jax.random.fold_in(splits[14], 71), 0)
    frozen_up_weight = draw_frozen_up_weight(jax.random.fold_in(splits[14], 71), 0)
    frozen_down_weight = draw_frozen_down_weight(jax.random.fold_in(splits[14], 71), 0)
    gate_left_factor = normal_values(splits[4], (MODEL_WIDTH, ADAPTER_RANK), MODEL_WIDTH ** -0.5, 0.0625, ((0, 16),))
    gate_right_factor = normal_values(splits[5], (ADAPTER_RANK, HIDDEN_UNITS), (4 * ADAPTER_RANK) ** -0.5, 0.75, ((1, 8),))
    up_left_factor = normal_values(splits[6], (MODEL_WIDTH, ADAPTER_RANK), MODEL_WIDTH ** -0.5, 0.0625, ((0, 16),))
    up_right_factor = normal_values(splits[7], (ADAPTER_RANK, HIDDEN_UNITS), (4 * ADAPTER_RANK) ** -0.5, 0.75, ((1, 8),))
    down_left_factor = normal_values(splits[8], (HIDDEN_UNITS, ADAPTER_RANK), HIDDEN_UNITS ** -0.5, 0.03125, ((0, 8),))
    down_right_factor = normal_values(splits[9], (ADAPTER_RANK, MODEL_WIDTH), (4 * ADAPTER_RANK) ** -0.5, 0.75, ((1, 16),))
    gate_column_magnitude = jnp.clip(jnp.exp(math.log(2.0) - 1.3862944 * jax.random.uniform(splits[10], (HIDDEN_UNITS,), jnp.float32) ** block_levels(splits[10], (HIDDEN_UNITS,), ((0, 8),), -0.2, 0.2)), 0.5, 2.0)
    up_column_magnitude = jnp.clip(jnp.exp(math.log(2.0) - 1.3862944 * jax.random.uniform(splits[11], (HIDDEN_UNITS,), jnp.float32) ** block_levels(splits[11], (HIDDEN_UNITS,), ((0, 8),), -0.2, 0.2)), 0.5, 2.0)
    down_column_magnitude = jnp.clip(jnp.exp(math.log(2.0) - 1.3862944 * jax.random.uniform(splits[12], (MODEL_WIDTH,), jnp.float32) ** block_levels(splits[12], (MODEL_WIDTH,), ((0, 16),), -0.2, 0.2)), 0.5, 2.0)
    cotangent = draw_cotangent(jax.random.fold_in(splits[14], 71), 0)
    return {"tokens": tokens, "frozen_gate_weight": frozen_gate_weight, "frozen_up_weight": frozen_up_weight, "frozen_down_weight": frozen_down_weight, "gate_left_factor": gate_left_factor, "gate_right_factor": gate_right_factor, "up_left_factor": up_left_factor, "up_right_factor": up_right_factor, "down_left_factor": down_left_factor, "down_right_factor": down_right_factor, "gate_column_magnitude": gate_column_magnitude, "up_column_magnitude": up_column_magnitude, "down_column_magnitude": down_column_magnitude, "cotangent": cotangent}


epsilon = 1e-06

def combine_adapter_columns(weight_matrix, left_factor, right_factor):
    combined_weight = weight_matrix.astype(jnp.float32) + jnp.dot(left_factor, right_factor, preferred_element_type=jnp.float32)
    norms = jnp.sqrt(lax.optimization_barrier(jnp.sum(combined_weight * combined_weight, axis=0)) + epsilon)
    return (combined_weight.astype(jnp.bfloat16), norms)

def blocked_product(left_side, right_side, blocks):
    inner = left_side.shape[1] // blocks
    left_blocks = left_side.reshape(left_side.shape[0], blocks, inner).transpose(1, 0, 2)
    right_blocks = right_side.reshape(blocks, inner, right_side.shape[1])

    def blocked_step(running, operands):
        partial_sum = jnp.dot(operands[0], operands[1], preferred_element_type=jnp.float32)
        rounded = lax.optimization_barrier(partial_sum.astype(jnp.bfloat16))
        return (running + rounded.astype(jnp.float32), None)
    start_value = jnp.zeros((left_side.shape[0], right_side.shape[1]), jnp.float32)
    running, _ = lax.scan(blocked_step, start_value, (left_blocks, right_blocks))
    return running

def reference(tokens, frozen_gate_weight, frozen_up_weight, frozen_down_weight, gate_left_factor, gate_right_factor, up_left_factor, up_right_factor, down_left_factor, down_right_factor, gate_column_magnitude, up_column_magnitude, down_column_magnitude, cotangent):
    gate_half_precision, gate_column_norm = combine_adapter_columns(frozen_gate_weight, gate_left_factor, gate_right_factor)
    up_half_precision, up_column_norm = combine_adapter_columns(frozen_up_weight, up_left_factor, up_right_factor)
    down_half_precision, down_column_norm = combine_adapter_columns(frozen_down_weight, down_left_factor, down_right_factor)
    scale_gate = gate_column_magnitude / gate_column_norm
    scale_up = up_column_magnitude / up_column_norm
    scale_down = down_column_magnitude / down_column_norm
    pre_gate = blocked_product(tokens, gate_half_precision, N_MP)
    pre_up = blocked_product(tokens, up_half_precision, N_MP)
    gate_act = pre_gate * scale_gate
    up_act = pre_up * scale_up
    sigmoid_gate = jax.nn.sigmoid(gate_act)
    silu_gate = gate_act * sigmoid_gate
    hidden_state = (silu_gate * up_act).astype(jnp.bfloat16)
    down_preactivation = jnp.dot(hidden_state, down_half_precision, preferred_element_type=jnp.float32)
    feedforward_output = (down_preactivation * scale_down).astype(jnp.bfloat16)
    output_cotangent = cotangent.astype(jnp.float32)
    down_logits = (output_cotangent * scale_down).astype(jnp.bfloat16)
    down_magnitude_gradient = lax.optimization_barrier(jnp.sum(output_cotangent * down_preactivation, axis=0)) / down_column_norm
    grad_hidden = blocked_product(down_logits, down_half_precision.T, N_MP)
    grad_gate = grad_hidden * up_act * sigmoid_gate * (1.0 + gate_act * (1.0 - sigmoid_gate))
    grad_up = grad_hidden * silu_gate
    gate_logits = (grad_gate * scale_gate).astype(jnp.bfloat16)
    up_logits = (grad_up * scale_up).astype(jnp.bfloat16)
    gate_magnitude_gradient = lax.optimization_barrier(jnp.sum(grad_gate * pre_gate, axis=0)) / gate_column_norm
    up_magnitude_gradient = lax.optimization_barrier(jnp.sum(grad_up * pre_up, axis=0)) / up_column_norm
    token_input_gradient = (jnp.dot(gate_logits, gate_half_precision.T, preferred_element_type=jnp.float32) + jnp.dot(up_logits, up_half_precision.T, preferred_element_type=jnp.float32)).astype(jnp.bfloat16)
    gate_projection_output = jnp.dot(tokens, gate_left_factor, preferred_element_type=jnp.float32).astype(jnp.bfloat16)
    up_projection_output = jnp.dot(tokens, up_left_factor, preferred_element_type=jnp.float32).astype(jnp.bfloat16)
    down_projection_output = jnp.dot(hidden_state, down_left_factor, preferred_element_type=jnp.float32).astype(jnp.bfloat16)
    gate_backward_rows = jnp.dot(gate_logits, gate_right_factor.T, preferred_element_type=jnp.float32).astype(jnp.bfloat16)
    up_backward_rows = jnp.dot(up_logits, up_right_factor.T, preferred_element_type=jnp.float32).astype(jnp.bfloat16)
    down_backward_rows = jnp.dot(down_logits, down_right_factor.T, preferred_element_type=jnp.float32).astype(jnp.bfloat16)
    gate_right_factor_gradient = jnp.dot(gate_projection_output.T, gate_logits, preferred_element_type=jnp.float32)
    up_right_factor_gradient = jnp.dot(up_projection_output.T, up_logits, preferred_element_type=jnp.float32)
    down_right_factor_gradient = jnp.dot(down_projection_output.T, down_logits, preferred_element_type=jnp.float32)
    gate_left_factor_gradient = jnp.dot(tokens.T, gate_backward_rows, preferred_element_type=jnp.float32)
    up_left_factor_gradient = jnp.dot(tokens.T, up_backward_rows, preferred_element_type=jnp.float32)
    down_left_factor_gradient = jnp.dot(hidden_state.T, down_backward_rows, preferred_element_type=jnp.float32)
    return (feedforward_output, token_input_gradient, gate_magnitude_gradient, up_magnitude_gradient, down_magnitude_gradient, gate_right_factor_gradient, gate_left_factor_gradient, up_right_factor_gradient, up_left_factor_gradient, down_right_factor_gradient, down_left_factor_gradient)
```

```python
import jax
import jax.numpy as jnp
from jax import lax
from jax.experimental import pallas as pl
from jax.experimental.pallas import tpu as pltpu
from jax.sharding import PartitionSpec as P

F32 = jnp.float32
BF16 = jnp.bfloat16
MESH = pl.DeviceIdType.MESH
EPS = 1e-06

GROUPS = 7
HALF = 256
STAGES = 9


def nn(a, b):
    return jnp.dot(a, b, preferred_element_type=F32)


def nt(a, b):
    return lax.dot_general(a, b, (((1,), (1,)), ((), ())), preferred_element_type=F32)


def kernel(
    tok, cot, wg_hbm, wu_hbm, wd_hbm, gl, gr, ul, ur, dl, dr, lt, dlt, gmag, umag, dmag,
    out, dx, ggm, gum, gdm, ggr, ggl, gur, gul, gdr, gdl,
    wg, wu, wd, gath, xt, zt, sqd_c, sqd_x, scd, nby, nbz, scl, nrm, pry, prz, pr,
    part, r1h, r1f, q, r2h, r2f, hz, mgy, mgz, oacc, xacc, bk,
    fs, fr, th, tf, smc, smx, mdc, mdx,
    wsem, ssem, rsem, ms, mr,
):
    dp = lax.axis_index("dp")
    mp = lax.axis_index("mp")
    x, c = dp // 2, dp % 2
    y, z = mp // 4, mp % 4

    def at_x(i):
        return (i * 2 + c, mp)

    def at_y(i):
        return (dp, i * 4 + z)

    def at_z(i):
        return (dp, y * 4 + i)

    other = (x * 2 + 1 - c, mp)

    def rcopy(src, dst, s, r, dev):
        return pltpu.make_async_remote_copy(
            src_ref=src, dst_ref=dst, send_sem=s, recv_sem=r, device_id=dev, device_id_type=MESH
        )

    def mcopy(src, dst, k, dev):
        return rcopy(src, dst, ms.at[k], mr.at[k], dev)

    def spread(slots, me, place, k):
        return [
            mcopy(slots.at[me], slots.at[me], k + d - 1, place((me + d) % 4)) for d in (1, 2, 3)
        ]

    def start(copies):
        for cp in copies:
            cp.start()

    def wait(copies):
        for cp in copies:
            cp.wait()

    def load_d(j, h):
        return pltpu.make_async_copy(
            wd_hbm.at[pl.ds(pl.multiple_of((j * 2 + h) * HALF, HALF), HALF)],
            wd.at[j, h],
            wsem.at[0, j, h],
        )

    def load_gu(w_hbm, w, k, j, h):
        return pltpu.make_async_copy(
            w_hbm.at[:, pl.ds(pl.multiple_of((j * 2 + h) * HALF, HALF), HALF)],
            w.at[j, h],
            wsem.at[k, j, h],
        )

    @pl.loop(0, GROUPS)
    def _(j):
        for h in (0, 1):
            load_d(j, h).start()

    @pl.loop(0, GROUPS)
    def _(j):
        for h in (0, 1):
            load_gu(wg_hbm, wg, 1, j, h).start()
            load_gu(wu_hbm, wu, 2, j, h).start()

    gath[x, c, 0] = tok[...]
    gath[x, c, 1] = cot[...]

    barrier = pltpu.get_barrier_semaphore()
    for d in (1, 2, 3):
        for dev in (at_x((x + d) % 4), at_y((y + d) % 4), at_z((z + d) % 4)):
            pl.semaphore_signal(barrier, inc=1, device_id=dev, device_id_type=MESH)
    pl.semaphore_signal(barrier, inc=1, device_id=other, device_id_type=MESH)
    pl.semaphore_wait(barrier, 10)

    xr, xl, xo = (x + 1) % 4, (x + 3) % 4, (x + 2) % 4
    own = gath.at[x, c]
    g_own = [
        mcopy(own, own, 0, at_x(xr)),
        mcopy(own, own, 1, at_x(xl)),
        mcopy(own, own, 2, other),
    ]
    start(g_own)

    def merge_down(j, total):
        for h in (0, 1):
            load_d(j, h).wait()
            rows = pl.ds(pl.multiple_of((j * 2 + h) * HALF, HALF), HALF)
            m = wd[j, h].astype(F32) + nn(dl[rows, :], dr[...])
            wd[j, h] = m.astype(BF16)
            total = total + jnp.sum(m * m, axis=0, keepdims=True)
        return total

    sqd_c[c] = lax.fori_loop(0, GROUPS, merge_down, jnp.zeros((1, 512), F32))
    s_core = mcopy(sqd_c.at[c], sqd_c.at[c], 3, other)
    s_core.start()

    wait(g_own[:2])
    lo, ro = gath.at[xl, c], gath.at[xr, c]
    g_fwd = [
        mcopy(gath.at[xl, c, 0], gath.at[xl, c, 0], 4, at_x(xr)),
        mcopy(gath.at[xr, c, 1], gath.at[xr, c, 1], 5, at_x(xl)),
        mcopy(lo, lo, 6, other),
        mcopy(ro, ro, 7, other),
    ]
    start(g_fwd)

    def merge_gu(k, w_hbm, w, left, right, j):
        for h in (0, 1):
            load_gu(w_hbm, w, k, j, h).wait()
            cols = pl.ds(pl.multiple_of((j * 2 + h) * HALF, HALF), HALF)
            m = w[j, h].astype(F32) + nn(left[...], right[:, cols])
            w[j, h] = m.astype(BF16)
            nby[y, k - 1 : k, cols] = jnp.sum(m * m, axis=0, keepdims=True)

    @pl.loop(0, GROUPS)
    def _(j):
        merge_gu(1, wg_hbm, wg, gl, gr, j)

    s_core.wait()
    sqd_x[x] = sqd_c[0] + sqd_c[1]
    s_x = spread(sqd_x, x, at_x, 8)
    start(s_x)
    wait(g_fwd[:2])
    oo = gath.at[xo, c]
    g_last = mcopy(oo, oo, 11, other)
    g_last.start()

    @pl.loop(0, GROUPS)
    def _(j):
        merge_gu(2, wu_hbm, wu, ul, ur, j)

    n_y = spread(nby, y, at_y, 12)
    start(n_y)

    wait(s_x)
    sqd = sqd_x[0] + sqd_x[1] + sqd_x[2] + sqd_x[3]
    normd = jnp.sqrt(sqd + EPS)
    scd[0:1] = normd
    scd[1:2] = dmag[...] / normd
    g_own[2].wait()
    wait(g_fwd[2:])
    g_last.wait()

    for b in range(16):
        px, pc, rows = b // 4, (b // 2) % 2, slice((b % 2) * 32, (b % 2) * 32 + 32)
        p = (b % 4) * 4 + b // 4
        t = gath[px, pc, 0, rows]
        v = (gath[px, pc, 1, rows].astype(F32) * scd[1:2]).astype(BF16)
        xt[0, b * 32 : b * 32 + 32] = t
        xt[1, p * 32 : p * 32 + 32] = t
        zt[0, b * 32 : b * 32 + 32] = v
        zt[1, p * 32 : p * 32 + 32] = v

    pry[y, 0:32] = nt(lt[...], xt[0]).astype(BF16)
    pry[y, 32:48] = nt(dr[...], zt[0]).astype(BF16)
    p_y = spread(pry, y, at_y, 18)
    start(p_y)
    n_z = spread(nbz, z, at_z, 15)
    p_z = spread(prz, z, at_z, 21)
    m_y = spread(mgy, y, at_y, 24)
    m_z = spread(mgz, z, at_z, 27)

    ri = lax.broadcasted_iota(jnp.int32, (512, 512), 0)
    ci = lax.broadcasted_iota(jnp.int32, (512, 512), 1)
    swapped = ((ri // 32) % 4) * 128 + (ri // 128) * 32 + ri % 32
    swap = (swapped == ci).astype(BF16)

    oacc[...] = jnp.zeros_like(oacc)
    xacc[...] = jnp.zeros_like(xacc)
    bk[...] = jnp.zeros_like(bk)

    def geometry(h):
        ia = y + h * (z - y)
        ib = z + h * (y - z)

        def at_a(i):
            return (dp, (i + h * (y - i)) * 4 + z + h * (i - z))

        def at_b(i):
            return (dp, (y + h * (i - y)) * 4 + i + h * (z - i))

        return ia, ib, at_a, at_b

    def copies(s, j, h):
        ia, ib, at_a, at_b = geometry(h)
        ar, al, ao = (ia + 1) % 4, (ia + 3) % 4, (ia + 2) % 4
        br, bl, bo = (ib + 1) % 4, (ib + 3) % 4, (ib + 2) % 4
        if s == 0:
            a = part.at[j, h, :, ao, 0:2], r1h.at[j, h, 0]
            b = part.at[j, h, :, ao, 2:4], r1h.at[j, h, 1]
        elif s == 1:
            a = part.at[j, h, :, ar], r1f.at[j, h, 0]
            b = part.at[j, h, :, al], r1f.at[j, h, 1]
        elif s == 2:
            a = q.at[j, h, :, bo, 0:16], r2h.at[j, h, 0]
            b = q.at[j, h, :, bo, 16:32], r2h.at[j, h, 1]
        elif s == 3:
            a = q.at[j, h, :, br], r2f.at[j, h, 0]
            b = q.at[j, h, :, bl], r2f.at[j, h, 1]
        elif s == 4:
            a = b = (hz.at[j, h, :, ia, ib],) * 2
        elif s == 5:
            a = (hz.at[j, h, :, ia, bl, 0:16],) * 2
            b = (hz.at[j, h, :, ia, br, 16:32],) * 2
        elif s == 6:
            a = b = (hz.at[j, h, :, ia],) * 2
        else:
            a = (hz.at[j, h, :, al, 0:2],) * 2
            b = (hz.at[j, h, :, ar, 2:4],) * 2
        if s in (0, 1, 6, 7):
            dr_, dl_ = at_a(ar), at_a(al)
        else:
            dr_, dl_ = at_b(br), at_b(bl)
        return [
            rcopy(*a, ssem.at[s, j, h, 0], rsem.at[s, j, h, 0], dr_),
            rcopy(*b, ssem.at[s, j, h, 1], rsem.at[s, j, h, 1], dl_),
        ]

    def add_into(ref, extra):
        ref[...] = (ref[...].astype(F32) + extra[...].astype(F32)).astype(BF16)

    def stage(s, j, h):
        ia, ib, _, _ = geometry(h)
        ar, al = (ia + 1) % 4, (ia + 3) % 4
        br, bl = (ib + 1) % 4, (ib + 3) % 4
        cols = pl.ds(pl.multiple_of((j * 2 + h) * HALF, HALF), HALF)
        if s > 0:
            wait(copies(s - 1, j, h))
        if s == 0:
            part[j, h, 0] = nn(xt[h], wg[j, h]).astype(BF16).reshape(4, 4, 32, HALF)
            part[j, h, 1] = nn(xt[h], wu[j, h]).astype(BF16).reshape(4, 4, 32, HALF)
            part[j, h, 2] = nt(zt[h], wd[j, h]).astype(BF16).reshape(4, 4, 32, HALF)
        elif s == 1:
            add_into(part.at[j, h, :, ar, 0:2], r1h.at[j, h, 0])
            add_into(part.at[j, h, :, al, 2:4], r1h.at[j, h, 1])
        elif s == 2:
            q[j, h] = (
                part[j, h, :, ia].astype(F32)
                + r1f[j, h, 0].astype(F32)
                + r1f[j, h, 1].astype(F32)
            ).astype(BF16)
        elif s == 3:
            add_into(q.at[j, h, :, br, 0:16], r2h.at[j, h, 0])
            add_into(q.at[j, h, :, bl, 16:32], r2h.at[j, h, 1])
        elif s == 4:
            pg, pu, gh = (
                q[j, h, k, ib].astype(F32) + r2f[j, h, 0, k].astype(F32) + r2f[j, h, 1, k].astype(F32)
                for k in range(3)
            )
            sg, su = scl[0:1, cols], scl[1:2, cols]
            ga, ua = pg * sg, pu * su
            sig = 1.0 / (1.0 + jnp.exp(-ga))
            silu = ga * sig
            dg = gh * ua * sig * (1.0 + ga * (1.0 - sig))
            du = gh * silu
            hz[j, h, 0, ia, ib] = (silu * ua).astype(BF16)
            hz[j, h, 1, ia, ib] = (dg * sg).astype(BF16)
            hz[j, h, 2, ia, ib] = (du * su).astype(BF16)
            mgy[y, 0:1, cols] = jnp.sum(dg * pg, axis=0, keepdims=True)
            mgy[y, 1:2, cols] = jnp.sum(du * pu, axis=0, keepdims=True)
        elif s == 8:
            hid = hz[j, h, 0].reshape(512, HALF)
            zg = hz[j, h, 1].reshape(512, HALF)
            zu = hz[j, h, 2].reshape(512, HALF)
            oacc[h] += nn(hid, wd[j, h])
            xacc[h] += nt(zg, wg[j, h]) + nt(zu, wu[j, h])
            ggr[:, cols] = nn(pr[h, 0:16], zg)
            gur[:, cols] = nn(pr[h, 16:32], zu)
            gdl[:, cols] = nn(pr[h, 32:48], hid)
            bk[h, 0:16] += nt(gr[:, cols], zg)
            bk[h, 16:32] += nt(ur[:, cols], zu)
            bk[h, 32:48] += nt(dlt[:, cols], hid)
        if s < 8:
            start(copies(s, j, h))

    @pl.loop(0, GROUPS + STAGES - 1)
    def _(t):
        @pl.when(t == 4)
        def _():
            wait(n_z)
            for k, mag in enumerate((gmag, umag)):
                n = jnp.sqrt(
                    nbz[0, k : k + 1] + nbz[1, k : k + 1] + nbz[2, k : k + 1] + nbz[3, k : k + 1] + EPS
                )
                nrm[k : k + 1] = n
                scl[k : k + 1] = mag[...] / n

        @pl.when(t == 7)
        def _():
            wait(p_z)
            total = sum(prz[k].astype(F32) for k in range(4)).astype(BF16)
            pr[0] = total
            pr[1] = nn(total, swap).astype(BF16)

        for s in range(STAGES):
            j = t - s

            @pl.when(jnp.logical_and(j >= 0, j < GROUPS))
            def _():
                @pl.loop(0, 2)
                def _(h):
                    stage(s, j, h)

        @pl.when(t == 0)
        def _():
            wait(n_y)
            nbz[z] = nby[0] + nby[1] + nby[2] + nby[3]
            start(n_z)

        @pl.when(t == 1)
        def _():
            wait(p_y)
            prz[z] = sum(pry[k].astype(F32) for k in range(4)).astype(BF16)
            start(p_z)

        @pl.when(t == GROUPS + 3)
        def _():
            start(m_y)

        @pl.when(t == GROUPS + 5)
        def _():
            wait(m_y)
            mgz[z] = mgy[0] + mgy[1] + mgy[2] + mgy[3]
            start(m_z)

    md = jnp.zeros((1, 512), F32)
    for b in range(16):
        px, pc, rows = b // 4, (b // 2) % 2, slice((b % 2) * 32, (b % 2) * 32 + 32)
        p = (b % 4) * 4 + b // 4
        o = oacc[0, b * 32 : b * 32 + 32] + oacc[1, p * 32 : p * 32 + 32]
        v = xacc[0, b * 32 : b * 32 + 32] + xacc[1, p * 32 : p * 32 + 32]
        md = md + jnp.sum(o * gath[px, pc, 1, rows].astype(F32), axis=0, keepdims=True)
        fs[pc, 0, px, rows] = o.astype(BF16)
        fs[pc, 1, px, rows] = v.astype(BF16)
    f_core = mcopy(fs.at[1 - c], fr, 30, other)
    f_core.start()
    mdc[c] = md
    smc[c] = (bk[0] + nn(bk[1].astype(BF16), swap)).astype(BF16)
    md_core = mcopy(mdc.at[c], mdc.at[c], 31, other)
    sm_core = mcopy(smc.at[c], smc.at[c], 32, other)
    start([md_core, sm_core])
    f_core.wait()
    add_into(fs.at[c], fr)
    f_half = [
        mcopy(fs.at[c, :, xo, 0:32], th.at[0], 33, at_x(xr)),
        mcopy(fs.at[c, :, xo, 32:64], th.at[1], 34, at_x(xl)),
    ]
    start(f_half)
    wait([md_core, sm_core])
    mdx[x] = mdc[0] + mdc[1]
    smx[x] = (smc[0].astype(F32) + smc[1].astype(F32)).astype(BF16)
    sm_x = spread(smx, x, at_x, 37)
    md_x = spread(mdx, x, at_x, 40)
    start(sm_x)
    start(md_x)
    wait(f_half)
    add_into(fs.at[c, :, xr, 0:32], th.at[0])
    add_into(fs.at[c, :, xl, 32:64], th.at[1])
    f_full = [
        mcopy(fs.at[c, :, xr], tf.at[0], 35, at_x(xr)),
        mcopy(fs.at[c, :, xl], tf.at[1], 36, at_x(xl)),
    ]
    start(f_full)

    wait(m_z)
    mags = (mgz[0] + mgz[1] + mgz[2] + mgz[3]) / nrm[...]
    ggm[...] = mags[0:1]
    gum[...] = mags[1:2]
    wait(sm_x)
    back = sum(smx[k].astype(F32) for k in range(4)).astype(BF16)
    lg = nn(back[0:32], xt[0])
    ggl[...] = lg[0:16]
    gul[...] = lg[16:32]
    gdr[...] = nn(back[32:48], zt[0])
    wait(md_x)
    gdm[...] = (mdx[0] + mdx[1] + mdx[2] + mdx[3]) / scd[0:1]
    wait(f_full)
    tot = fs[c, :, x].astype(F32) + tf[0].astype(F32) + tf[1].astype(F32)
    out[...] = (tot[0] * scd[1:2]).astype(BF16)
    dx[...] = tot[1].astype(BF16)


def per_device(tok, fg, fu, fd, gl, gr, ul, ur, dl, dr, gmag, umag, dmag, cot):
    vm = pl.BlockSpec(memory_space=pltpu.VMEM)
    hbm = pl.BlockSpec(memory_space=pl.ANY)
    f = jax.ShapeDtypeStruct
    V = pltpu.VMEM
    G, C = GROUPS, HALF
    lt = jnp.concatenate([gl.T, ul.T], axis=0)
    call = pl.pallas_call(
        kernel,
        out_shape=(
            f((64, 512), BF16), f((64, 512), BF16),
            f((1, 3584), F32), f((1, 3584), F32), f((1, 512), F32),
            f((16, 3584), F32), f((16, 512), F32), f((16, 3584), F32), f((16, 512), F32),
            f((16, 512), F32), f((16, 3584), F32),
        ),
        in_specs=[vm, vm, hbm, hbm, hbm] + [vm] * 11,
        out_specs=(vm,) * 11,
        scratch_shapes=[
            V((G, 2, 512, C), BF16), V((G, 2, 512, C), BF16), V((G, 2, C, 512), BF16),
            V((4, 2, 2, 64, 512), BF16), V((2, 512, 512), BF16), V((2, 512, 512), BF16),
            V((2, 1, 512), F32), V((4, 1, 512), F32), V((2, 512), F32),
            V((4, 2, 3584), F32), V((4, 2, 3584), F32), V((2, 3584), F32), V((2, 3584), F32),
            V((4, 48, 512), BF16), V((4, 48, 512), BF16), V((2, 48, 512), BF16),
            V((G, 2, 3, 4, 4, 32, C), BF16),
            V((G, 2, 2, 3, 2, 32, C), BF16), V((G, 2, 2, 3, 4, 32, C), BF16),
            V((G, 2, 3, 4, 32, C), BF16),
            V((G, 2, 2, 3, 16, C), BF16), V((G, 2, 2, 3, 32, C), BF16),
            V((G, 2, 3, 4, 4, 32, C), BF16),
            V((4, 2, 3584), F32), V((4, 2, 3584), F32),
            V((2, 512, 512), F32), V((2, 512, 512), F32), V((2, 48, 512), F32),
            V((2, 2, 4, 64, 512), BF16), V((2, 4, 64, 512), BF16),
            V((2, 2, 32, 512), BF16), V((2, 2, 64, 512), BF16),
            V((2, 48, 512), BF16), V((4, 48, 512), BF16),
            V((2, 1, 512), F32), V((4, 1, 512), F32),
            pltpu.SemaphoreType.DMA((3, G, 2)),
            pltpu.SemaphoreType.DMA((8, G, 2, 2)),
            pltpu.SemaphoreType.DMA((8, G, 2, 2)),
            pltpu.SemaphoreType.DMA((43,)),
            pltpu.SemaphoreType.DMA((43,)),
        ],
        compiler_params=pltpu.CompilerParams(
            collective_id=0, has_side_effects=True, vmem_limit_bytes=63 * 1024 * 1024
        ),
    )
    o, d, ggm, gum, gdm, ggr, ggl, gur, gul, gdr, gdl = call(
        tok, cot, fg, fu, fd, gl, gr, ul, ur, dl, dr, lt, dl.T,
        gmag.reshape(1, -1), umag.reshape(1, -1), dmag.reshape(1, -1),
    )
    return (
        o, d, ggm.reshape(-1), gum.reshape(-1), gdm.reshape(-1),
        ggr, ggl.T, gur, gul.T, gdr, gdl.T,
    )


def solution(mesh):
    in_specs = (
        P("dp", "mp"), P("mp", "dp"), P("mp", "dp"), P("dp", "mp"),
        P("mp", None), P(None, "dp"), P("mp", None), P(None, "dp"),
        P("dp", None), P(None, "mp"), P("dp"), P("dp"), P("mp"), P("dp", "mp"),
    )
    out_specs = (
        P("dp", "mp"), P("dp", "mp"), P("dp"), P("dp"), P("mp"),
        P(None, "dp"), P("mp", None), P(None, "dp"), P("mp", None), P(None, "mp"), P("dp", None),
    )
    return jax.shard_map(
        per_device, mesh=mesh, in_specs=in_specs, out_specs=out_specs, check_vma=False
    )
```

```python
import jax
import jax.numpy as jnp
from jax import lax
from jax.experimental import pallas as pl
from jax.experimental.pallas import tpu as pltpu
from jax.sharding import PartitionSpec as P

F32 = jnp.float32
BF16 = jnp.bfloat16
MESH = pl.DeviceIdType.MESH
EPS = 1e-06

GROUPS = 7
HALF = 256
STAGES = 9


def nn(a, b):
    return jnp.dot(a, b, preferred_element_type=F32)


def nt(a, b):
    return lax.dot_general(a, b, (((1,), (1,)), ((), ())), preferred_element_type=F32)


def tn(a, b):
    return lax.dot_general(a, b, (((0,), (0,)), ((), ())), preferred_element_type=F32)


def kernel(
    tok, cot, wg_hbm, wu_hbm, wd_hbm, glt, gr, ult, ur, dlt, dr, gmag, umag, dmag,
    out, dx, ggm, gum, gdm, ggr, ggl, gur, gul, gdr, gdl,
    wg, wu, wd, gath, xt, zt, sqd_c, sqd_x, scd, nby, nbz, scl, nrm, pry, prz, pr,
    part, r1h, r1f, q, r2h, r2f, hz, mgy, mgz, oacc, xacc, bk,
    fs, fr, th, tf, smc, smx, mdc, mdx,
    wsem, ssem, rsem, ms, mr,
):
    dp = lax.axis_index("dp")
    mp = lax.axis_index("mp")
    x, c = dp // 2, dp % 2
    y, z = mp // 4, mp % 4

    def at_x(i):
        return (i * 2 + c, mp)

    def at_y(i):
        return (dp, i * 4 + z)

    def at_z(i):
        return (dp, y * 4 + i)

    other = (x * 2 + 1 - c, mp)

    def rcopy(src, dst, s, r, dev):
        return pltpu.make_async_remote_copy(
            src_ref=src, dst_ref=dst, send_sem=s, recv_sem=r, device_id=dev, device_id_type=MESH
        )

    def mcopy(src, dst, k, dev):
        return rcopy(src, dst, ms.at[k], mr.at[k], dev)

    def spread(slots, me, place, k):
        return [
            mcopy(slots.at[me], slots.at[me], k + d - 1, place((me + d) % 4)) for d in (1, 2, 3)
        ]

    def start(copies):
        for cp in copies:
            cp.start()

    def wait(copies):
        for cp in copies:
            cp.wait()

    def load_d(j, h):
        return pltpu.make_async_copy(
            wd_hbm.at[pl.ds(pl.multiple_of((j * 2 + h) * HALF, HALF), HALF)],
            wd.at[j, h],
            wsem.at[0, j, h],
        )

    def load_gu(w_hbm, w, k, j, h):
        return pltpu.make_async_copy(
            w_hbm.at[:, pl.ds(pl.multiple_of((j * 2 + h) * HALF, HALF), HALF)],
            w.at[j, h],
            wsem.at[k, j, h],
        )

    @pl.loop(0, GROUPS)
    def _(j):
        for h in (0, 1):
            load_d(j, h).start()

    @pl.loop(0, GROUPS)
    def _(j):
        for h in (0, 1):
            load_gu(wg_hbm, wg, 1, j, h).start()
            load_gu(wu_hbm, wu, 2, j, h).start()

    gath[x, c, 0] = tok[...]
    gath[x, c, 1] = cot[...]

    barrier = pltpu.get_barrier_semaphore()
    for d in (1, 2, 3):
        for dev in (at_x((x + d) % 4), at_y((y + d) % 4), at_z((z + d) % 4)):
            pl.semaphore_signal(barrier, inc=1, device_id=dev, device_id_type=MESH)
    pl.semaphore_signal(barrier, inc=1, device_id=other, device_id_type=MESH)
    pl.semaphore_wait(barrier, 10)

    xr, xl, xo = (x + 1) % 4, (x + 3) % 4, (x + 2) % 4
    own = gath.at[x, c]
    g_own = [
        mcopy(own, own, 0, at_x(xr)),
        mcopy(own, own, 1, at_x(xl)),
        mcopy(own, own, 2, other),
    ]
    start(g_own)

    def merge_down(j, total):
        for h in (0, 1):
            load_d(j, h).wait()
            rows = pl.ds(pl.multiple_of((j * 2 + h) * HALF, HALF), HALF)
            m = wd[j, h].astype(F32) + tn(dlt[:, rows], dr[...])
            wd[j, h] = m.astype(BF16)
            total = total + jnp.sum(m * m, axis=0, keepdims=True)
        return total

    sqd_c[c] = lax.fori_loop(0, GROUPS, merge_down, jnp.zeros((1, 512), F32))
    s_core = mcopy(sqd_c.at[c], sqd_c.at[c], 3, other)
    s_core.start()

    wait(g_own[:2])
    lo, ro = gath.at[xl, c], gath.at[xr, c]
    g_fwd = [
        mcopy(gath.at[xl, c, 0], gath.at[xl, c, 0], 4, at_x(xr)),
        mcopy(gath.at[xr, c, 1], gath.at[xr, c, 1], 5, at_x(xl)),
        mcopy(lo, lo, 6, other),
        mcopy(ro, ro, 7, other),
    ]
    start(g_fwd)

    def merge_gu(k, w_hbm, w, left, right, j):
        for h in (0, 1):
            load_gu(w_hbm, w, k, j, h).wait()
            cols = pl.ds(pl.multiple_of((j * 2 + h) * HALF, HALF), HALF)
            m = w[j, h].astype(F32) + tn(left[...], right[:, cols])
            w[j, h] = m.astype(BF16)
            nby[y, k - 1 : k, cols] = jnp.sum(m * m, axis=0, keepdims=True)

    @pl.loop(0, GROUPS)
    def _(j):
        merge_gu(1, wg_hbm, wg, glt, gr, j)

    s_core.wait()
    sqd_x[x] = sqd_c[0] + sqd_c[1]
    s_x = spread(sqd_x, x, at_x, 8)
    start(s_x)
    wait(g_fwd[:2])
    oo = gath.at[xo, c]
    g_last = mcopy(oo, oo, 11, other)
    g_last.start()

    @pl.loop(0, GROUPS)
    def _(j):
        merge_gu(2, wu_hbm, wu, ult, ur, j)

    n_y = spread(nby, y, at_y, 12)
    start(n_y)

    wait(s_x)
    sqd = sqd_x[0] + sqd_x[1] + sqd_x[2] + sqd_x[3]
    normd = jnp.sqrt(sqd + EPS)
    scd[0:1] = normd
    scd[1:2] = dmag[...].reshape(1, 512) / normd
    g_own[2].wait()
    wait(g_fwd[2:])
    g_last.wait()

    for b in range(16):
        px, pc, rows = b // 4, (b // 2) % 2, slice((b % 2) * 32, (b % 2) * 32 + 32)
        p = (b % 4) * 4 + b // 4
        t = gath[px, pc, 0, rows]
        v = (gath[px, pc, 1, rows].astype(F32) * scd[1:2]).astype(BF16)
        xt[0, b * 32 : b * 32 + 32] = t
        xt[1, p * 32 : p * 32 + 32] = t
        zt[0, b * 32 : b * 32 + 32] = v
        zt[1, p * 32 : p * 32 + 32] = v

    pry[y, 0:16] = nt(glt[...], xt[0]).astype(BF16)
    pry[y, 16:32] = nt(ult[...], xt[0]).astype(BF16)
    pry[y, 32:48] = nt(dr[...], zt[0]).astype(BF16)
    p_y = spread(pry, y, at_y, 18)
    start(p_y)
    n_z = spread(nbz, z, at_z, 15)
    p_z = spread(prz, z, at_z, 21)
    m_y = spread(mgy, y, at_y, 24)
    m_z = spread(mgz, z, at_z, 27)

    ri = lax.broadcasted_iota(jnp.int32, (512, 512), 0)
    ci = lax.broadcasted_iota(jnp.int32, (512, 512), 1)
    swapped = ((ri // 32) % 4) * 128 + (ri // 128) * 32 + ri % 32
    swap = (swapped == ci).astype(BF16)

    oacc[...] = jnp.zeros_like(oacc)
    xacc[...] = jnp.zeros_like(xacc)
    bk[...] = jnp.zeros_like(bk)

    def geometry(h):
        ia = y + h * (z - y)
        ib = z + h * (y - z)

        def at_a(i):
            return (dp, (i + h * (y - i)) * 4 + z + h * (i - z))

        def at_b(i):
            return (dp, (y + h * (i - y)) * 4 + i + h * (z - i))

        return ia, ib, at_a, at_b

    def copies(s, j, h):
        ia, ib, at_a, at_b = geometry(h)
        ar, al, ao = (ia + 1) % 4, (ia + 3) % 4, (ia + 2) % 4
        br, bl, bo = (ib + 1) % 4, (ib + 3) % 4, (ib + 2) % 4
        if s == 0:
            a = part.at[j, h, :, ao, 0:2], r1h.at[j, h, 0]
            b = part.at[j, h, :, ao, 2:4], r1h.at[j, h, 1]
        elif s == 1:
            a = part.at[j, h, :, ar], r1f.at[j, h, 0]
            b = part.at[j, h, :, al], r1f.at[j, h, 1]
        elif s == 2:
            a = q.at[j, h, :, bo, 0:16], r2h.at[j, h, 0]
            b = q.at[j, h, :, bo, 16:32], r2h.at[j, h, 1]
        elif s == 3:
            a = q.at[j, h, :, br], r2f.at[j, h, 0]
            b = q.at[j, h, :, bl], r2f.at[j, h, 1]
        elif s == 4:
            a = b = (hz.at[j, h, :, ia, ib],) * 2
        elif s == 5:
            a = (hz.at[j, h, :, ia, bl, 0:16],) * 2
            b = (hz.at[j, h, :, ia, br, 16:32],) * 2
        elif s == 6:
            a = b = (hz.at[j, h, :, ia],) * 2
        else:
            a = (hz.at[j, h, :, al, 0:2],) * 2
            b = (hz.at[j, h, :, ar, 2:4],) * 2
        if s in (0, 1, 6, 7):
            dr_, dl_ = at_a(ar), at_a(al)
        else:
            dr_, dl_ = at_b(br), at_b(bl)
        return [
            rcopy(*a, ssem.at[s, j, h, 0], rsem.at[s, j, h, 0], dr_),
            rcopy(*b, ssem.at[s, j, h, 1], rsem.at[s, j, h, 1], dl_),
        ]

    def add_into(ref, extra):
        ref[...] = (ref[...].astype(F32) + extra[...].astype(F32)).astype(BF16)

    def stage(s, j, h):
        ia, ib, _, _ = geometry(h)
        ar, al = (ia + 1) % 4, (ia + 3) % 4
        br, bl = (ib + 1) % 4, (ib + 3) % 4
        cols = pl.ds(pl.multiple_of((j * 2 + h) * HALF, HALF), HALF)
        if s > 0:
            wait(copies(s - 1, j, h))
        if s == 0:
            part[j, h, 0] = nn(xt[h], wg[j, h]).astype(BF16).reshape(4, 4, 32, HALF)
            part[j, h, 1] = nn(xt[h], wu[j, h]).astype(BF16).reshape(4, 4, 32, HALF)
            part[j, h, 2] = nt(zt[h], wd[j, h]).astype(BF16).reshape(4, 4, 32, HALF)
        elif s == 1:
            add_into(part.at[j, h, :, ar, 0:2], r1h.at[j, h, 0])
            add_into(part.at[j, h, :, al, 2:4], r1h.at[j, h, 1])
        elif s == 2:
            q[j, h] = (
                part[j, h, :, ia].astype(F32)
                + r1f[j, h, 0].astype(F32)
                + r1f[j, h, 1].astype(F32)
            ).astype(BF16)
        elif s == 3:
            add_into(q.at[j, h, :, br, 0:16], r2h.at[j, h, 0])
            add_into(q.at[j, h, :, bl, 16:32], r2h.at[j, h, 1])
        elif s == 4:
            pg, pu, gh = (
                q[j, h, k, ib].astype(F32) + r2f[j, h, 0, k].astype(F32) + r2f[j, h, 1, k].astype(F32)
                for k in range(3)
            )
            sg, su = scl[0:1, cols], scl[1:2, cols]
            ga, ua = pg * sg, pu * su
            sig = 1.0 / (1.0 + jnp.exp(-ga))
            silu = ga * sig
            dg = gh * ua * sig * (1.0 + ga * (1.0 - sig))
            du = gh * silu
            hz[j, h, 0, ia, ib] = (silu * ua).astype(BF16)
            hz[j, h, 1, ia, ib] = (dg * sg).astype(BF16)
            hz[j, h, 2, ia, ib] = (du * su).astype(BF16)
            mgy[y, 0:1, cols] = jnp.sum(dg * pg, axis=0, keepdims=True)
            mgy[y, 1:2, cols] = jnp.sum(du * pu, axis=0, keepdims=True)
        elif s == 8:
            hid = hz[j, h, 0].reshape(512, HALF)
            zg = hz[j, h, 1].reshape(512, HALF)
            zu = hz[j, h, 2].reshape(512, HALF)
            oacc[h] += nn(hid, wd[j, h])
            xacc[h] += nt(zg, wg[j, h]) + nt(zu, wu[j, h])
            ggr[:, cols] = nn(pr[h, 0:16], zg)
            gur[:, cols] = nn(pr[h, 16:32], zu)
            gdl[:, cols] = nn(pr[h, 32:48], hid)
            bk[h, 0:16] += nt(gr[:, cols], zg)
            bk[h, 16:32] += nt(ur[:, cols], zu)
            bk[h, 32:48] += nt(dlt[:, cols], hid)
        if s < 8:
            start(copies(s, j, h))

    @pl.loop(0, GROUPS + STAGES - 1)
    def _(t):
        @pl.when(t == 4)
        def _():
            wait(n_z)
            for k, mag in enumerate((gmag, umag)):
                n = jnp.sqrt(
                    nbz[0, k : k + 1] + nbz[1, k : k + 1] + nbz[2, k : k + 1] + nbz[3, k : k + 1] + EPS
                )
                nrm[k : k + 1] = n
                scl[k : k + 1] = mag[...].reshape(1, 3584) / n

        @pl.when(t == 7)
        def _():
            wait(p_z)
            total = sum(prz[k].astype(F32) for k in range(4)).astype(BF16)
            pr[0] = total
            pr[1] = nn(total, swap).astype(BF16)

        for s in range(STAGES):
            j = t - s

            @pl.when(jnp.logical_and(j >= 0, j < GROUPS))
            def _():
                @pl.loop(0, 2)
                def _(h):
                    stage(s, j, h)

        @pl.when(t == 0)
        def _():
            wait(n_y)
            nbz[z] = nby[0] + nby[1] + nby[2] + nby[3]
            start(n_z)

        @pl.when(t == 1)
        def _():
            wait(p_y)
            prz[z] = sum(pry[k].astype(F32) for k in range(4)).astype(BF16)
            start(p_z)

        @pl.when(t == GROUPS + 3)
        def _():
            start(m_y)

        @pl.when(t == GROUPS + 5)
        def _():
            wait(m_y)
            mgz[z] = mgy[0] + mgy[1] + mgy[2] + mgy[3]
            start(m_z)

    md = jnp.zeros((1, 512), F32)
    for b in range(16):
        px, pc, rows = b // 4, (b // 2) % 2, slice((b % 2) * 32, (b % 2) * 32 + 32)
        p = (b % 4) * 4 + b // 4
        o = oacc[0, b * 32 : b * 32 + 32] + oacc[1, p * 32 : p * 32 + 32]
        v = xacc[0, b * 32 : b * 32 + 32] + xacc[1, p * 32 : p * 32 + 32]
        md = md + jnp.sum(o * gath[px, pc, 1, rows].astype(F32), axis=0, keepdims=True)
        fs[pc, 0, px, rows] = o.astype(BF16)
        fs[pc, 1, px, rows] = v.astype(BF16)
    f_core = mcopy(fs.at[1 - c], fr, 30, other)
    f_core.start()
    mdc[c] = md
    smc[c] = (bk[0] + nn(bk[1].astype(BF16), swap)).astype(BF16)
    md_core = mcopy(mdc.at[c], mdc.at[c], 31, other)
    sm_core = mcopy(smc.at[c], smc.at[c], 32, other)
    start([md_core, sm_core])
    f_core.wait()
    add_into(fs.at[c], fr)
    f_half = [
        mcopy(fs.at[c, :, xo, 0:32], th.at[0], 33, at_x(xr)),
        mcopy(fs.at[c, :, xo, 32:64], th.at[1], 34, at_x(xl)),
    ]
    start(f_half)
    wait([md_core, sm_core])
    mdx[x] = mdc[0] + mdc[1]
    smx[x] = (smc[0].astype(F32) + smc[1].astype(F32)).astype(BF16)
    sm_x = spread(smx, x, at_x, 37)
    md_x = spread(mdx, x, at_x, 40)
    start(sm_x)
    start(md_x)
    wait(f_half)
    add_into(fs.at[c, :, xr, 0:32], th.at[0])
    add_into(fs.at[c, :, xl, 32:64], th.at[1])
    f_full = [
        mcopy(fs.at[c, :, xr], tf.at[0], 35, at_x(xr)),
        mcopy(fs.at[c, :, xl], tf.at[1], 36, at_x(xl)),
    ]
    start(f_full)

    wait(m_z)
    mags = (mgz[0] + mgz[1] + mgz[2] + mgz[3]) / nrm[...]
    ggm[...] = mags[0:1]
    gum[...] = mags[1:2]
    wait(sm_x)
    back = sum(smx[k].astype(F32) for k in range(4)).astype(BF16)
    lg = nn(back[0:32], xt[0])
    ggl[...] = lg[0:16]
    gul[...] = lg[16:32]
    gdr[...] = nn(back[32:48], zt[0])
    wait(md_x)
    gdm[...] = (mdx[0] + mdx[1] + mdx[2] + mdx[3]) / scd[0:1]
    wait(f_full)
    tot = fs[c, :, x].astype(F32) + tf[0].astype(F32) + tf[1].astype(F32)
    out[...] = (tot[0] * scd[1:2]).astype(BF16)
    dx[...] = tot[1].astype(BF16)


def per_device(tok, fg, fu, fd, gl, gr, ul, ur, dl, dr, gmag, umag, dmag, cot):
    vm = pl.BlockSpec(memory_space=pltpu.VMEM)
    hbm = pl.BlockSpec(memory_space=pl.ANY)
    f = jax.ShapeDtypeStruct
    V = pltpu.VMEM
    G, C = GROUPS, HALF
    call = pl.pallas_call(
        kernel,
        out_shape=(
            f((64, 512), BF16), f((64, 512), BF16),
            f((1, 3584), F32), f((1, 3584), F32), f((1, 512), F32),
            f((16, 3584), F32), f((16, 512), F32), f((16, 3584), F32), f((16, 512), F32),
            f((16, 512), F32), f((16, 3584), F32),
        ),
        in_specs=[vm, vm, hbm, hbm, hbm] + [vm] * 9,
        out_specs=(vm,) * 11,
        scratch_shapes=[
            V((G, 2, 512, C), BF16), V((G, 2, 512, C), BF16), V((G, 2, C, 512), BF16),
            V((4, 2, 2, 64, 512), BF16), V((2, 512, 512), BF16), V((2, 512, 512), BF16),
            V((2, 1, 512), F32), V((4, 1, 512), F32), V((2, 512), F32),
            V((4, 2, 3584), F32), V((4, 2, 3584), F32), V((2, 3584), F32), V((2, 3584), F32),
            V((4, 48, 512), BF16), V((4, 48, 512), BF16), V((2, 48, 512), BF16),
            V((G, 2, 3, 4, 4, 32, C), BF16),
            V((G, 2, 2, 3, 2, 32, C), BF16), V((G, 2, 2, 3, 4, 32, C), BF16),
            V((G, 2, 3, 4, 32, C), BF16),
            V((G, 2, 2, 3, 16, C), BF16), V((G, 2, 2, 3, 32, C), BF16),
            V((G, 2, 3, 4, 4, 32, C), BF16),
            V((4, 2, 3584), F32), V((4, 2, 3584), F32),
            V((2, 512, 512), F32), V((2, 512, 512), F32), V((2, 48, 512), F32),
            V((2, 2, 4, 64, 512), BF16), V((2, 4, 64, 512), BF16),
            V((2, 2, 32, 512), BF16), V((2, 2, 64, 512), BF16),
            V((2, 48, 512), BF16), V((4, 48, 512), BF16),
            V((2, 1, 512), F32), V((4, 1, 512), F32),
            pltpu.SemaphoreType.DMA((3, G, 2)),
            pltpu.SemaphoreType.DMA((8, G, 2, 2)),
            pltpu.SemaphoreType.DMA((8, G, 2, 2)),
            pltpu.SemaphoreType.DMA((43,)),
            pltpu.SemaphoreType.DMA((43,)),
        ],
        compiler_params=pltpu.CompilerParams(
            collective_id=0, has_side_effects=True, vmem_limit_bytes=63 * 1024 * 1024
        ),
    )
    res = call(tok, cot, fg, fu, fd, gl.T, gr, ul.T, ur, dl.T, dr, gmag, umag, dmag)
    flat = (2, 3, 4)

    def finish(*refs):
        for k in range(11):
            value = refs[k][...]
            refs[k + 11][...] = value.reshape(-1) if k in flat else value

    o, d, ggm, gum, gdm, ggr, ggl, gur, gul, gdr, gdl = pl.pallas_call(
        finish,
        out_shape=tuple(
            f((r.size,) if k in flat else r.shape, r.dtype) for k, r in enumerate(res)
        ),
        in_specs=[vm] * 11,
        out_specs=(vm,) * 11,
    )(*res)
    return o, d, ggm, gum, gdm, ggr, ggl.T, gur, gul.T, gdr, gdl.T


def solution(mesh):
    in_specs = (
        P("dp", "mp"), P("mp", "dp"), P("mp", "dp"), P("dp", "mp"),
        P("mp", None), P(None, "dp"), P("mp", None), P(None, "dp"),
        P("dp", None), P(None, "mp"), P("dp"), P("dp"), P("mp"), P("dp", "mp"),
    )
    out_specs = (
        P("dp", "mp"), P("dp", "mp"), P("dp"), P("dp"), P("mp"),
        P(None, "dp"), P("mp", None), P(None, "dp"), P("mp", None), P(None, "mp"), P("dp", None),
    )
    return jax.shard_map(
        per_device, mesh=mesh, in_specs=in_specs, out_specs=out_specs, check_vma=False
    )
```

```python
import jax
import jax.numpy as jnp
from jax import lax
from jax.experimental import pallas as pl
from jax.experimental.pallas import tpu as pltpu
from jax.sharding import PartitionSpec as P

F32 = jnp.float32
BF16 = jnp.bfloat16
MESH = pl.DeviceIdType.MESH
EPS = 1e-06

GROUPS = 7
HALF = 256
STAGES = 9


def nn(a, b):
    return jnp.dot(a, b, preferred_element_type=F32)


def nt(a, b):
    return lax.dot_general(a, b, (((1,), (1,)), ((), ())), preferred_element_type=F32)


def tn(a, b):
    return lax.dot_general(a, b, (((0,), (0,)), ((), ())), preferred_element_type=F32)


def kernel(
    tok, cot, wg_hbm, wu_hbm, wd_hbm, glt, gr, ult, ur, dlt, dr, gmag, umag, dmag,
    out, dx, ggm, gum, gdm, ggr, ggl, gur, gul, gdr, gdl,
    wg, wu, wd, gath, xt, zt, sqd_c, sqd_x, scd, nby, nbz, scl, nrm, pry, prz, pr,
    part, r1h, r1f, q, r2h, r2f, hz, mgy, mgz, oacc, xacc, bk,
    fs, fr, th, tf, smc, smx, mdc, mdx,
    wsem, ssem, rsem, ms, mr, spread_s, spread_r,
):
    dp = lax.axis_index("dp")
    mp = lax.axis_index("mp")
    x, c = dp // 2, dp % 2
    y, z = mp // 4, mp % 4

    def at_x(i):
        return (i * 2 + c, mp)

    def at_y(i):
        return (dp, i * 4 + z)

    def at_z(i):
        return (dp, y * 4 + i)

    other = (x * 2 + 1 - c, mp)

    def rcopy(src, dst, s, r, dev):
        return pltpu.make_async_remote_copy(
            src_ref=src, dst_ref=dst, send_sem=s, recv_sem=r, device_id=dev, device_id_type=MESH
        )

    def mcopy(src, dst, k, dev):
        return rcopy(src, dst, ms.at[k], mr.at[k], dev)

    def landed(ref, sem):
        pltpu.make_async_copy(ref, ref, sem).wait()

    def spread(slots, me, place, k):
        for d in (1, 2, 3):
            rcopy(
                slots.at[me], slots.at[me], spread_s.at[k], spread_r.at[k], place((me + d) % 4)
            ).start()

    def spread_wait(slots, k):
        landed(slots.at[0:3], spread_s.at[k])
        landed(slots.at[0:3], spread_r.at[k])

    def ring_own(slots, me, place, k):
        for i in ((me + 1) % 4, (me + 3) % 4):
            rcopy(slots.at[me], slots.at[me], spread_s.at[k], spread_r.at[k], place(i)).start()

    def ring_pass(slots, me, place, k):
        landed(slots.at[0:2], spread_s.at[k])
        landed(slots.at[0:2], spread_r.at[k])
        half = slots.shape[2] // 2
        right, left = (me + 1) % 4, (me + 3) % 4
        a, b = slots.at[left, :, 0:half], slots.at[right, :, half:]
        rcopy(a, a, spread_s.at[k + 1], spread_r.at[k + 1], place(right)).start()
        rcopy(b, b, spread_s.at[k + 1], spread_r.at[k + 1], place(left)).start()

    def ring_wait(slots, k):
        landed(slots.at[0], spread_s.at[k + 1])
        landed(slots.at[0], spread_r.at[k + 1])

    def start(copies):
        for cp in copies:
            cp.start()

    def wait(copies):
        for cp in copies:
            cp.wait()

    def load_d(j, h):
        return pltpu.make_async_copy(
            wd_hbm.at[pl.ds(pl.multiple_of((j * 2 + h) * HALF, HALF), HALF)],
            wd.at[j, h],
            wsem.at[0, j],
        )

    def load_gu(w_hbm, w, k, j, h):
        return pltpu.make_async_copy(
            w_hbm.at[:, pl.ds(pl.multiple_of((j * 2 + h) * HALF, HALF), HALF)],
            w.at[j, h],
            wsem.at[k, j],
        )

    @pl.loop(0, GROUPS)
    def _(j):
        for h in (0, 1):
            load_d(j, h).start()

    @pl.loop(0, GROUPS)
    def _(j):
        for h in (0, 1):
            load_gu(wg_hbm, wg, 1, j, h).start()
            load_gu(wu_hbm, wu, 2, j, h).start()

    gath[x, c, 0] = tok[...]
    gath[x, c, 1] = cot[...]

    barrier = pltpu.get_barrier_semaphore()
    for d in (1, 2, 3):
        for dev in (at_x((x + d) % 4), at_y((y + d) % 4), at_z((z + d) % 4)):
            pl.semaphore_signal(barrier, inc=1, device_id=dev, device_id_type=MESH)
    pl.semaphore_signal(barrier, inc=1, device_id=other, device_id_type=MESH)
    pl.semaphore_wait(barrier, 10)

    xr, xl, xo = (x + 1) % 4, (x + 3) % 4, (x + 2) % 4
    own = gath.at[x, c]
    g_own = [
        mcopy(own, own, 0, at_x(xr)),
        mcopy(own, own, 1, at_x(xl)),
        mcopy(own, own, 2, other),
    ]
    start(g_own)

    def merge_down(j, total):
        landed(wd.at[j], wsem.at[0, j])
        for h in (0, 1):
            rows = pl.ds(pl.multiple_of((j * 2 + h) * HALF, HALF), HALF)
            m = wd[j, h].astype(F32) + tn(dlt[:, rows], dr[...])
            wd[j, h] = m.astype(BF16)
            total = total + jnp.sum(m * m, axis=0, keepdims=True)
        return total

    sqd_c[c] = lax.fori_loop(0, GROUPS, merge_down, jnp.zeros((1, 512), F32))
    s_core = mcopy(sqd_c.at[c], sqd_c.at[c], 3, other)
    s_core.start()

    wait(g_own[:2])
    lo, ro = gath.at[xl, c], gath.at[xr, c]
    g_fwd = [
        mcopy(gath.at[xl, c, 0], gath.at[xl, c, 0], 4, at_x(xr)),
        mcopy(gath.at[xr, c, 1], gath.at[xr, c, 1], 5, at_x(xl)),
        mcopy(lo, lo, 6, other),
        mcopy(ro, ro, 7, other),
    ]
    start(g_fwd)

    def merge_gu(j):
        for k, w, left, right in ((0, wg, glt, gr), (1, wu, ult, ur)):
            landed(w.at[j], wsem.at[k + 1, j])
            for h in (0, 1):
                cols = pl.ds(pl.multiple_of((j * 2 + h) * HALF, HALF), HALF)
                m = w[j, h].astype(F32) + tn(left[...], right[:, cols])
                w[j, h] = m.astype(BF16)
                nby[y, k : k + 1, cols] = jnp.sum(m * m, axis=0, keepdims=True)

    s_core.wait()
    sqd_x[x] = sqd_c[0] + sqd_c[1]
    spread(sqd_x, x, at_x, 0)
    wait(g_fwd[:2])
    oo = gath.at[xo, c]
    g_last = mcopy(oo, oo, 8, other)
    g_last.start()
    merge_gu(0)

    spread_wait(sqd_x, 0)
    sqd = sqd_x[0] + sqd_x[1] + sqd_x[2] + sqd_x[3]
    normd = jnp.sqrt(sqd + EPS)
    scd[0:1] = normd
    scd[1:2] = dmag[...].reshape(1, 512) / normd
    g_own[2].wait()
    wait(g_fwd[2:])
    g_last.wait()

    for b in range(16):
        px, pc, rows = b // 4, (b // 2) % 2, slice((b % 2) * 32, (b % 2) * 32 + 32)
        p = (b % 4) * 4 + b // 4
        t = gath[px, pc, 0, rows]
        v = (gath[px, pc, 1, rows].astype(F32) * scd[1:2]).astype(BF16)
        xt[0, b * 32 : b * 32 + 32] = t
        xt[1, p * 32 : p * 32 + 32] = t
        zt[0, b * 32 : b * 32 + 32] = v
        zt[1, p * 32 : p * 32 + 32] = v

    def swap():
        ri = lax.broadcasted_iota(jnp.int32, (512, 512), 0)
        ci = lax.broadcasted_iota(jnp.int32, (512, 512), 1)
        swapped = ((ri // 32) % 4) * 128 + (ri // 128) * 32 + ri % 32
        return (swapped == ci).astype(BF16)

    def geometry(h):
        ia = y + h * (z - y)
        ib = z + h * (y - z)

        def at_a(i):
            return (dp, (i + h * (y - i)) * 4 + z + h * (i - z))

        def at_b(i):
            return (dp, (y + h * (i - y)) * 4 + i + h * (z - i))

        return ia, ib, at_a, at_b

    def copies(s, j, h):
        ia, ib, at_a, at_b = geometry(h)
        ar, al, ao = (ia + 1) % 4, (ia + 3) % 4, (ia + 2) % 4
        br, bl, bo = (ib + 1) % 4, (ib + 3) % 4, (ib + 2) % 4
        if s == 0:
            a = part.at[j, h, :, ao, 0:2], r1h.at[j, h, 0]
            b = part.at[j, h, :, ao, 2:4], r1h.at[j, h, 1]
        elif s == 1:
            a = part.at[j, h, :, ar], r1f.at[j, h, 0]
            b = part.at[j, h, :, al], r1f.at[j, h, 1]
        elif s == 2:
            a = q.at[j, h, :, bo, 0:16], r2h.at[j, h, 0]
            b = q.at[j, h, :, bo, 16:32], r2h.at[j, h, 1]
        elif s == 3:
            a = q.at[j, h, :, br], r2f.at[j, h, 0]
            b = q.at[j, h, :, bl], r2f.at[j, h, 1]
        elif s == 4:
            a = b = (hz.at[j, h, :, ia, ib],) * 2
        elif s == 5:
            a = (hz.at[j, h, :, ia, bl, 0:16],) * 2
            b = (hz.at[j, h, :, ia, br, 16:32],) * 2
        elif s == 6:
            a = b = (hz.at[j, h, :, ia],) * 2
        else:
            a = (hz.at[j, h, :, al, 0:2],) * 2
            b = (hz.at[j, h, :, ar, 2:4],) * 2
        if s in (0, 1, 6, 7):
            dr_, dl_ = at_a(ar), at_a(al)
        else:
            dr_, dl_ = at_b(br), at_b(bl)
        return [
            rcopy(*a, ssem.at[s, j % 3, h], rsem.at[s, j % 3, h], dr_),
            rcopy(*b, ssem.at[s, j % 3, h], rsem.at[s, j % 3, h], dl_),
        ]

    def arrived(s, j, h):
        both = (
            r1h.at[j, h], r1f.at[j, h], r2h.at[j, h], r2f.at[j, h],
            hz.at[j, h, :, 0, 0:2], hz.at[j, h, :, 0, 0], hz.at[j, h, :, 0:2], hz.at[j, h, :, 0],
        )[s]
        landed(both, ssem.at[s, j % 3, h])
        landed(both, rsem.at[s, j % 3, h])

    def add_into(ref, extra):
        ref[...] = (ref[...].astype(F32) + extra[...].astype(F32)).astype(BF16)

    def stage(s, j, h):
        ia, ib, _, _ = geometry(h)
        ar, al = (ia + 1) % 4, (ia + 3) % 4
        br, bl = (ib + 1) % 4, (ib + 3) % 4
        cols = pl.ds(pl.multiple_of((j * 2 + h) * HALF, HALF), HALF)
        if s > 0:
            arrived(s - 1, j, h)
        if s == 0:
            part[j, h, 0] = nn(xt[h], wg[j, h]).astype(BF16).reshape(4, 4, 32, HALF)
            part[j, h, 1] = nn(xt[h], wu[j, h]).astype(BF16).reshape(4, 4, 32, HALF)
            part[j, h, 2] = nt(zt[h], wd[j, h]).astype(BF16).reshape(4, 4, 32, HALF)
        elif s == 1:
            add_into(part.at[j, h, :, ar, 0:2], r1h.at[j, h, 0])
            add_into(part.at[j, h, :, al, 2:4], r1h.at[j, h, 1])
        elif s == 2:
            q[j, h] = (
                part[j, h, :, ia].astype(F32)
                + r1f[j, h, 0].astype(F32)
                + r1f[j, h, 1].astype(F32)
            ).astype(BF16)
        elif s == 3:
            add_into(q.at[j, h, :, br, 0:16], r2h.at[j, h, 0])
            add_into(q.at[j, h, :, bl, 16:32], r2h.at[j, h, 1])
        elif s == 4:
            pg, pu, gh = (
                q[j, h, k, ib].astype(F32) + r2f[j, h, 0, k].astype(F32) + r2f[j, h, 1, k].astype(F32)
                for k in range(3)
            )
            sg, su = scl[0:1, cols], scl[1:2, cols]
            ga, ua = pg * sg, pu * su
            sig = 1.0 / (1.0 + jnp.exp(-ga))
            silu = ga * sig
            dg = gh * ua * sig * (1.0 + ga * (1.0 - sig))
            du = gh * silu
            hz[j, h, 0, ia, ib] = (silu * ua).astype(BF16)
            hz[j, h, 1, ia, ib] = (dg * sg).astype(BF16)
            hz[j, h, 2, ia, ib] = (du * su).astype(BF16)
            mgy[y, 0:1, cols] = jnp.sum(dg * pg, axis=0, keepdims=True)
            mgy[y, 1:2, cols] = jnp.sum(du * pu, axis=0, keepdims=True)
        elif s == 8:
            hid = hz[j, h, 0].reshape(512, HALF)
            zg = hz[j, h, 1].reshape(512, HALF)
            zu = hz[j, h, 2].reshape(512, HALF)
            oacc[h] += nn(hid, wd[j, h])
            xacc[h] += nt(zg, wg[j, h]) + nt(zu, wu[j, h])
            ggr[:, cols] = nn(pr[h, 0:16], zg)
            gur[:, cols] = nn(pr[h, 16:32], zu)
            gdl[:, cols] = nn(pr[h, 32:48], hid)
            bk[h, 0:16] += nt(gr[:, cols], zg)
            bk[h, 16:32] += nt(ur[:, cols], zu)
            bk[h, 32:48] += nt(dlt[:, cols], hid)
        if s < 8:
            start(copies(s, j, h))

    @pl.loop(0, GROUPS + STAGES - 1)
    def _(t):
        for s in range(STAGES):
            j = t - s
            if s == 4:

                @pl.when(t == 4)
                def _():
                    spread_wait(nbz, 2)
                    for k, mag in enumerate((gmag, umag)):
                        row = slice(k, k + 1)
                        n = jnp.sqrt(nbz[0, row] + nbz[1, row] + nbz[2, row] + nbz[3, row] + EPS)
                        nrm[row] = n
                        scl[row] = mag[...].reshape(1, 3584) / n

            @pl.when(jnp.logical_and(j >= 0, j < GROUPS))
            def _():
                @pl.loop(0, 2)
                def _(h):
                    stage(s, j, h)

        @pl.when(t < 3)
        def _():
            merge_gu(2 * t + 1)
            merge_gu(2 * t + 2)

        @pl.when(t == 1)
        def _():
            pry[y, 0:16] = nt(glt[...], xt[0]).astype(BF16)
            pry[y, 16:32] = nt(ult[...], xt[0]).astype(BF16)
            pry[y, 32:48] = nt(dr[...], zt[0]).astype(BF16)
            ring_own(pry, y, at_y, 3)

        @pl.when(t == 2)
        def _():
            spread(nby, y, at_y, 1)
            ring_pass(pry, y, at_y, 3)

        @pl.when(t == 3)
        def _():
            oacc[...] = jnp.zeros_like(oacc)
            xacc[...] = jnp.zeros_like(xacc)
            bk[...] = jnp.zeros_like(bk)
            spread_wait(nby, 1)
            nbz[z] = nby[0] + nby[1] + nby[2] + nby[3]
            spread(nbz, z, at_z, 2)

        @pl.when(t == 4)
        def _():
            ring_wait(pry, 3)
            prz[z] = sum(pry[k].astype(F32) for k in range(4)).astype(BF16)
            ring_own(prz, z, at_z, 5)

        @pl.when(t == 5)
        def _():
            ring_pass(prz, z, at_z, 5)

        @pl.when(t == 6)
        def _():
            ring_wait(prz, 5)
            total = sum(prz[k].astype(F32) for k in range(4)).astype(BF16)
            pr[0] = total
            pr[1] = nn(total, swap()).astype(BF16)

        @pl.when(t == GROUPS + 3)
        def _():
            ring_own(mgy, y, at_y, 7)

        @pl.when(t == GROUPS + 4)
        def _():
            ring_pass(mgy, y, at_y, 7)

        @pl.when(t == GROUPS + 5)
        def _():
            ring_wait(mgy, 7)
            mgz[z] = mgy[0] + mgy[1] + mgy[2] + mgy[3]
            ring_own(mgz, z, at_z, 9)

        @pl.when(t == GROUPS + 6)
        def _():
            ring_pass(mgz, z, at_z, 9)

    md = jnp.zeros((1, 512), F32)
    for b in range(16):
        px, pc, rows = b // 4, (b // 2) % 2, slice((b % 2) * 32, (b % 2) * 32 + 32)
        p = (b % 4) * 4 + b // 4
        o = oacc[0, b * 32 : b * 32 + 32] + oacc[1, p * 32 : p * 32 + 32]
        v = xacc[0, b * 32 : b * 32 + 32] + xacc[1, p * 32 : p * 32 + 32]
        md = md + jnp.sum(o * gath[px, pc, 1, rows].astype(F32), axis=0, keepdims=True)
        fs[pc, 0, px, rows] = o.astype(BF16)
        fs[pc, 1, px, rows] = v.astype(BF16)
    f_core = mcopy(fs.at[1 - c], fr, 9, other)
    f_core.start()
    mdc[c] = md
    smc[c] = (bk[0] + nn(bk[1].astype(BF16), swap())).astype(BF16)
    md_core = mcopy(mdc.at[c], mdc.at[c], 10, other)
    sm_core = mcopy(smc.at[c], smc.at[c], 11, other)
    start([md_core, sm_core])
    f_core.wait()
    add_into(fs.at[c], fr)
    f_half = [
        mcopy(fs.at[c, :, xo, 0:32], th.at[0], 12, at_x(xr)),
        mcopy(fs.at[c, :, xo, 32:64], th.at[1], 13, at_x(xl)),
    ]
    start(f_half)
    wait([md_core, sm_core])
    mdx[x] = mdc[0] + mdc[1]
    smx[x] = (smc[0].astype(F32) + smc[1].astype(F32)).astype(BF16)
    ring_own(smx, x, at_x, 11)
    spread(mdx, x, at_x, 13)
    wait(f_half)
    add_into(fs.at[c, :, xr, 0:32], th.at[0])
    add_into(fs.at[c, :, xl, 32:64], th.at[1])
    f_full = [
        mcopy(fs.at[c, :, xr], tf.at[0], 14, at_x(xr)),
        mcopy(fs.at[c, :, xl], tf.at[1], 15, at_x(xl)),
    ]
    start(f_full)
    ring_pass(smx, x, at_x, 11)

    ring_wait(mgz, 9)
    mags = (mgz[0] + mgz[1] + mgz[2] + mgz[3]) / nrm[...]
    ggm[...] = mags[0:1]
    gum[...] = mags[1:2]
    ring_wait(smx, 11)
    back = sum(smx[k].astype(F32) for k in range(4)).astype(BF16)
    lg = nn(back[0:32], xt[0])
    ggl[...] = lg[0:16]
    gul[...] = lg[16:32]
    gdr[...] = nn(back[32:48], zt[0])
    spread_wait(mdx, 13)
    gdm[...] = (mdx[0] + mdx[1] + mdx[2] + mdx[3]) / scd[0:1]
    wait(f_full)
    tot = fs[c, :, x].astype(F32) + tf[0].astype(F32) + tf[1].astype(F32)
    out[...] = (tot[0] * scd[1:2]).astype(BF16)
    dx[...] = tot[1].astype(BF16)


def per_device(tok, fg, fu, fd, gl, gr, ul, ur, dl, dr, gmag, umag, dmag, cot):
    vm = pl.BlockSpec(memory_space=pltpu.VMEM)
    hbm = pl.BlockSpec(memory_space=pl.ANY)
    f = jax.ShapeDtypeStruct
    V = pltpu.VMEM
    G, C = GROUPS, HALF
    call = pl.pallas_call(
        kernel,
        out_shape=(
            f((64, 512), BF16), f((64, 512), BF16),
            f((1, 3584), F32), f((1, 3584), F32), f((1, 512), F32),
            f((16, 3584), F32), f((16, 512), F32), f((16, 3584), F32), f((16, 512), F32),
            f((16, 512), F32), f((16, 3584), F32),
        ),
        in_specs=[vm, vm, hbm, hbm, hbm] + [vm] * 9,
        out_specs=(vm,) * 11,
        scratch_shapes=[
            V((G, 2, 512, C), BF16), V((G, 2, 512, C), BF16), V((G, 2, C, 512), BF16),
            V((4, 2, 2, 64, 512), BF16), V((2, 512, 512), BF16), V((2, 512, 512), BF16),
            V((2, 1, 512), F32), V((4, 1, 512), F32), V((2, 512), F32),
            V((4, 2, 3584), F32), V((4, 2, 3584), F32), V((2, 3584), F32), V((2, 3584), F32),
            V((4, 48, 512), BF16), V((4, 48, 512), BF16), V((2, 48, 512), BF16),
            V((G, 2, 3, 4, 4, 32, C), BF16),
            V((G, 2, 2, 3, 2, 32, C), BF16), V((G, 2, 2, 3, 4, 32, C), BF16),
            V((G, 2, 3, 4, 32, C), BF16),
            V((G, 2, 2, 3, 16, C), BF16), V((G, 2, 2, 3, 32, C), BF16),
            V((G, 2, 3, 4, 4, 32, C), BF16),
            V((4, 2, 3584), F32), V((4, 2, 3584), F32),
            V((2, 512, 512), F32), V((2, 512, 512), F32), V((2, 48, 512), F32),
            V((2, 2, 4, 64, 512), BF16), V((2, 4, 64, 512), BF16),
            V((2, 2, 32, 512), BF16), V((2, 2, 64, 512), BF16),
            V((2, 48, 512), BF16), V((4, 48, 512), BF16),
            V((2, 1, 512), F32), V((4, 1, 512), F32),
            pltpu.SemaphoreType.DMA((3, G)),
            pltpu.SemaphoreType.DMA((8, 3, 2)),
            pltpu.SemaphoreType.DMA((8, 3, 2)),
            pltpu.SemaphoreType.DMA((16,)),
            pltpu.SemaphoreType.DMA((16,)),
            pltpu.SemaphoreType.DMA((14,)),
            pltpu.SemaphoreType.DMA((14,)),
        ],
        compiler_params=pltpu.CompilerParams(
            collective_id=0, has_side_effects=True, vmem_limit_bytes=63 * 1024 * 1024
        ),
    )
    res = call(tok, cot, fg, fu, fd, gl.T, gr, ul.T, ur, dl.T, dr, gmag, umag, dmag)
    flat = (2, 3, 4)

    def finish(*refs):
        for k in range(11):
            value = refs[k][...]
            refs[k + 11][...] = value.reshape(-1) if k in flat else value

    o, d, ggm, gum, gdm, ggr, ggl, gur, gul, gdr, gdl = pl.pallas_call(
        finish,
        out_shape=tuple(
            f((r.size,) if k in flat else r.shape, r.dtype) for k, r in enumerate(res)
        ),
        in_specs=[vm] * 11,
        out_specs=(vm,) * 11,
    )(*res)
    return o, d, ggm, gum, gdm, ggr, ggl.T, gur, gul.T, gdr, gdl.T


def solution(mesh):
    in_specs = (
        P("dp", "mp"), P("mp", "dp"), P("mp", "dp"), P("dp", "mp"),
        P("mp", None), P(None, "dp"), P("mp", None), P(None, "dp"),
        P("dp", None), P(None, "mp"), P("dp"), P("dp"), P("mp"), P("dp", "mp"),
    )
    out_specs = (
        P("dp", "mp"), P("dp", "mp"), P("dp"), P("dp"), P("mp"),
        P(None, "dp"), P("mp", None), P(None, "dp"), P("mp", None), P(None, "mp"), P("dp", None),
    )
    return jax.shard_map(
        per_device, mesh=mesh, in_specs=in_specs, out_specs=out_specs, check_vma=False
    )
```

```python
import jax
import jax.numpy as jnp
from jax import lax
from jax.experimental import pallas as pl
from jax.experimental.pallas import tpu as pltpu
from jax.sharding import PartitionSpec as P

F32 = jnp.float32
BF16 = jnp.bfloat16
MESH = pl.DeviceIdType.MESH
EPS = 1e-06

GROUPS = 7
HALF = 256
STAGES = 9


def nn(a, b):
    return jnp.dot(a, b, preferred_element_type=F32)


def nt(a, b):
    return lax.dot_general(a, b, (((1,), (1,)), ((), ())), preferred_element_type=F32)


def tn(a, b):
    return lax.dot_general(a, b, (((0,), (0,)), ((), ())), preferred_element_type=F32)


def kernel(
    tok, cot, wg_hbm, wu_hbm, wd_hbm, glt, gr, ult, ur, dlt, dr, gmag, umag, dmag,
    out, dx, ggm, gum, gdm, ggr, ggl, gur, gul, gdr, gdl,
    wg, wu, wd, gath, zt, sqd_c, sqd_x, scd, nf, nby, nbz, scl, nrm, lpad, dpad, pry, prz, pd, pr,
    part, r1h, r1f, q, r2h, r2f, hz, mf, mgy, mgz, oacc, xacc, bk,
    fs, fr, th, tf, smd, smy, back, mdc, mdx,
    wsem, ssem, rsem, ms, mr, spread_s, spread_r,
):
    dp = lax.axis_index("dp")
    mp = lax.axis_index("mp")
    x, c = dp // 2, dp % 2
    y, z = mp // 4, mp % 4

    def at_x(i):
        return (i * 2 + c, mp)

    def at_y(i):
        return (dp, i * 4 + z)

    def at_z(i):
        return (dp, y * 4 + i)

    def at_x_other(i):
        return (i * 2 + 1 - c, mp)

    other = at_x_other(x)

    def rcopy(src, dst, s, r, dev):
        return pltpu.make_async_remote_copy(
            src_ref=src, dst_ref=dst, send_sem=s, recv_sem=r, device_id=dev, device_id_type=MESH
        )

    def mcopy(src, dst, k, dev):
        return rcopy(src, dst, ms.at[k], mr.at[k], dev)

    def landed(ref, sem):
        pltpu.make_async_copy(ref, ref, sem).wait()

    def spread(slots, me, place, k):
        for d in (1, 2, 3):
            rcopy(
                slots.at[me], slots.at[me], spread_s.at[k], spread_r.at[k], place((me + d) % 4)
            ).start()

    def spread_wait(slots, k):
        landed(slots.at[0:3], spread_s.at[k])
        landed(slots.at[0:3], spread_r.at[k])

    def ring_own(slots, me, place, k):
        for i in ((me + 1) % 4, (me + 3) % 4):
            rcopy(slots.at[me], slots.at[me], spread_s.at[k], spread_r.at[k], place(i)).start()

    def ring_pass(slots, me, place, k):
        landed(slots.at[0:2], spread_s.at[k])
        landed(slots.at[0:2], spread_r.at[k])
        axis = 2 if slots.shape[2] > 128 else 1
        half = slots.shape[axis] // 2
        right, left = (me + 1) % 4, (me + 3) % 4
        if axis == 2:
            a, b = slots.at[left, :, 0:half], slots.at[right, :, half:]
        else:
            a, b = slots.at[left, 0:half], slots.at[right, half:]
        rcopy(a, a, spread_s.at[k + 1], spread_r.at[k + 1], place(right)).start()
        rcopy(b, b, spread_s.at[k + 1], spread_r.at[k + 1], place(left)).start()

    def ring_wait(slots, k):
        landed(slots.at[0], spread_s.at[k + 1])
        landed(slots.at[0], spread_r.at[k + 1])

    def start(copies):
        for cp in copies:
            cp.start()

    def wait(copies):
        for cp in copies:
            cp.wait()

    def load_d(j, h):
        return pltpu.make_async_copy(
            wd_hbm.at[pl.ds(pl.multiple_of((j * 2 + h) * HALF, HALF), HALF)],
            wd.at[j, h],
            wsem.at[0, j],
        )

    def load_gu(w_hbm, w, k, j, h):
        return pltpu.make_async_copy(
            w_hbm.at[:, pl.ds(pl.multiple_of((j * 2 + h) * HALF, HALF), HALF)],
            w.at[j, h],
            wsem.at[k, j],
        )

    @pl.loop(0, GROUPS)
    def _(j):
        for h in (0, 1):
            load_d(j, h).start()

    @pl.loop(0, GROUPS)
    def _(j):
        for h in (0, 1):
            load_gu(wg_hbm, wg, 1, j, h).start()
            load_gu(wu_hbm, wu, 2, j, h).start()

    gath[0, x, c] = tok[...]
    gath[1, x, c] = cot[...]

    barrier = pltpu.get_barrier_semaphore()
    for d in (1, 2, 3):
        for dev in (at_x((x + d) % 4), at_y((y + d) % 4), at_z((z + d) % 4)):
            pl.semaphore_signal(barrier, inc=1, device_id=dev, device_id_type=MESH)
    for dev in (other, *(at_x_other((x + d) % 4) for d in (1, 2, 3))):
        pl.semaphore_signal(barrier, inc=1, device_id=dev, device_id_type=MESH)
    pl.semaphore_wait(barrier, 13)

    xr, xl, xo = (x + 1) % 4, (x + 3) % 4, (x + 2) % 4
    own = gath.at[:, x, c]
    g_own = [
        mcopy(own, own, 0, at_x(xr)),
        mcopy(own, own, 1, at_x(xl)),
        mcopy(own, own, 2, other),
    ]
    start(g_own)

    def merge_down(j, total):
        landed(wd.at[j], wsem.at[0, j])
        for h in (0, 1):
            rows = pl.ds(pl.multiple_of((j * 2 + h) * HALF, HALF), HALF)
            m = wd[j, h].astype(F32) + tn(dlt[:, rows], dr[...])
            wd[j, h] = m.astype(BF16)
            total = total + jnp.sum(m * m, axis=0, keepdims=True)
        return total

    sqd_c[c] = lax.fori_loop(0, GROUPS, merge_down, jnp.zeros((1, 512), F32))
    s_core = mcopy(sqd_c.at[c], sqd_c.at[c], 3, other)
    s_core.start()

    wait(g_own[:2])
    lo, ro = gath.at[:, xl, c], gath.at[:, xr, c]
    a, b = gath.at[:, xl, c, 0:32], gath.at[:, xr, c, 32:64]
    g_fwd = [
        mcopy(a, a, 4, at_x(xr)),
        mcopy(b, b, 5, at_x(xl)),
        mcopy(a, a, 6, at_x_other(xr)),
        mcopy(b, b, 7, at_x_other(xl)),
        mcopy(lo, lo, 8, other),
        mcopy(ro, ro, 16, other),
    ]
    start(g_fwd)

    def merge_gu(j):
        for k, w, left, right in ((0, wg, glt, gr), (1, wu, ult, ur)):
            landed(w.at[j], wsem.at[k + 1, j])
            for h in (0, 1):
                cols = pl.ds(pl.multiple_of((j * 2 + h) * HALF, HALF), HALF)
                m = w[j, h].astype(F32) + tn(left[...], right[:, cols])
                w[j, h] = m.astype(BF16)
                nf[pl.ds(k * 8 + j, 1), h * HALF : (h + 1) * HALF] = jnp.sum(m * m, axis=0, keepdims=True)

    s_core.wait()
    sqd_x[x] = sqd_c[0] + sqd_c[1]
    spread(sqd_x, x, at_x, 0)
    merge_gu(0)

    spread_wait(sqd_x, 0)
    sqd = sqd_x[0] + sqd_x[1] + sqd_x[2] + sqd_x[3]
    normd = jnp.sqrt(sqd + EPS)
    scd[0:1] = normd
    scd[1:2] = dmag[...].reshape(1, 512) / normd
    g_own[2].wait()
    wait(g_fwd)

    nf[7:8] = jnp.ones((1, 512), F32)
    nf[15:16] = jnp.ones((1, 512), F32)
    scl[...] = jnp.ones_like(scl)
    mf[...] = jnp.zeros_like(mf)

    def tokens():
        return gath[0].reshape(512, 512)

    zt[...] = (gath[1].reshape(512, 512).astype(F32) * scd[1:2]).astype(BF16)

    def geometry(h):
        ia = y + h * (z - y)
        ib = z + h * (y - z)

        def at_a(i):
            return (dp, (i + h * (y - i)) * 4 + z + h * (i - z))

        def at_b(i):
            return (dp, (y + h * (i - y)) * 4 + i + h * (z - i))

        return ia, ib, at_a, at_b

    def copies(s, j, h):
        ia, ib, at_a, at_b = geometry(h)
        ar, al, ao = (ia + 1) % 4, (ia + 3) % 4, (ia + 2) % 4
        br, bl, bo = (ib + 1) % 4, (ib + 3) % 4, (ib + 2) % 4
        if s == 0:
            a = part.at[j, h, :, ao, 0:2], r1h.at[j, h, 0]
            b = part.at[j, h, :, ao, 2:4], r1h.at[j, h, 1]
        elif s == 1:
            a = part.at[j, h, :, ar], r1f.at[j, h, 0]
            b = part.at[j, h, :, al], r1f.at[j, h, 1]
        elif s == 2:
            a = q.at[j, h, :, bo, 0:16], r2h.at[j, h, 0]
            b = q.at[j, h, :, bo, 16:32], r2h.at[j, h, 1]
        elif s == 3:
            a = q.at[j, h, :, br], r2f.at[j, h, 0]
            b = q.at[j, h, :, bl], r2f.at[j, h, 1]
        elif s == 4:
            a = b = (hz.at[j, h, :, ia, ib],) * 2
        elif s == 5:
            a = (hz.at[j, h, :, ia, bl, 0:16],) * 2
            b = (hz.at[j, h, :, ia, br, 16:32],) * 2
        elif s == 6:
            a = b = (hz.at[j, h, :, ia],) * 2
        else:
            a = (hz.at[j, h, :, al, 0:2],) * 2
            b = (hz.at[j, h, :, ar, 2:4],) * 2
        if s in (0, 1, 6, 7):
            dr_, dl_ = at_a(ar), at_a(al)
        else:
            dr_, dl_ = at_b(br), at_b(bl)
        return [
            rcopy(*a, ssem.at[s, j % 2, h], rsem.at[s, j % 3, h], dr_),
            rcopy(*b, ssem.at[s, j % 2, h], rsem.at[s, j % 3, h], dl_),
        ]

    def arrived(s, j, h):
        both = (
            r1h.at[j, h], r1f.at[j, h], r2h.at[j, h], r2f.at[j, h],
            hz.at[j, h, :, 0, 0:2], hz.at[j, h, :, 0, 0], hz.at[j, h, :, 0:2], hz.at[j, h, :, 0],
        )[s]
        landed(both, ssem.at[s, j % 2, h])
        landed(both, rsem.at[s, j % 3, h])

    def add_into(ref, extra):
        ref[...] = (ref[...].astype(F32) + extra[...].astype(F32)).astype(BF16)

    def stage(s, j, h):
        ia, ib, _, _ = geometry(h)
        ar, al = (ia + 1) % 4, (ia + 3) % 4
        br, bl = (ib + 1) % 4, (ib + 3) % 4
        cols = pl.ds(pl.multiple_of((j * 2 + h) * HALF, HALF), HALF)
        if 0 < s < 9:
            arrived(s - 1, j, h)
        if s == 0:
            part[j, h, 0] = nn(tokens(), wg[j, h]).astype(BF16).reshape(4, 4, 32, HALF)
            part[j, h, 1] = nn(tokens(), wu[j, h]).astype(BF16).reshape(4, 4, 32, HALF)
            part[j, h, 2] = nt(zt[...], wd[j, h]).astype(BF16).reshape(4, 4, 32, HALF)
        elif s == 1:
            add_into(part.at[j, h, :, ar, 0:2], r1h.at[j, h, 0])
            add_into(part.at[j, h, :, al, 2:4], r1h.at[j, h, 1])
        elif s == 2:
            q[j, h] = (
                part[j, h, :, ia].astype(F32)
                + r1f[j, h, 0].astype(F32)
                + r1f[j, h, 1].astype(F32)
            ).astype(BF16)
        elif s == 3:
            add_into(q.at[j, h, :, br, 0:16], r2h.at[j, h, 0])
            add_into(q.at[j, h, :, bl, 16:32], r2h.at[j, h, 1])
        elif s == 4:
            pg, pu, gh = (
                q[j, h, k, ib].astype(F32) + r2f[j, h, 0, k].astype(F32) + r2f[j, h, 1, k].astype(F32)
                for k in range(3)
            )
            local = pl.ds(pl.multiple_of(h * HALF, HALF), HALF)
            sg, su = scl[pl.ds(j, 1), local], scl[pl.ds(8 + j, 1), local]
            ga, ua = pg * sg, pu * su
            sig = 1.0 / (1.0 + jnp.exp(-ga))
            silu = ga * sig
            dg = gh * ua * sig * (1.0 + ga * (1.0 - sig))
            du = gh * silu
            hz[j, h, 0, ia, ib] = (silu * ua).astype(BF16)
            hz[j, h, 1, ia, ib] = (dg * sg).astype(BF16)
            hz[j, h, 2, ia, ib] = (du * su).astype(BF16)
            mf[pl.ds(j, 1), local] = jnp.sum(dg * pg, axis=0, keepdims=True)
            mf[pl.ds(8 + j, 1), local] = jnp.sum(du * pu, axis=0, keepdims=True)
        elif s == 8:
            hid = hz[j, h, 0].reshape(512, HALF)
            oacc[...] += nn(hid, wd[j, h])
            gdl[:, cols] = nn(pr[32:48], hid)
            bk[32:48] += nt(dlt[:, cols], hid)
        elif s == 9:
            zg = hz[j, h, 1].reshape(512, HALF)
            zu = hz[j, h, 2].reshape(512, HALF)
            xacc[...] += nt(zg, wg[j, h]) + nt(zu, wu[j, h])
            ggr[:, cols] = nn(pr[0:16], zg)
            gur[:, cols] = nn(pr[16:32], zu)
            bk[0:16] += nt(gr[:, cols], zg)
            bk[16:32] += nt(ur[:, cols], zu)
        if s < 8:
            start(copies(s, j, h))

    own_pd = pd.at[x, c]
    pd_core = mcopy(own_pd, own_pd, 22, other)
    pd_right = mcopy(own_pd, own_pd, 23, at_x(xr))
    pd_left = mcopy(own_pd, own_pd, 24, at_x(xl))
    lo_pd, ro_pd, oo_pd = pd.at[xl, c], pd.at[xr, c], pd.at[xo, c]
    a_pd, b_pd = pd.at[xl, c, 0:32], pd.at[xr, c, 32:64]
    pd_pass = [
        mcopy(a_pd, a_pd, 25, at_x(xr)),
        mcopy(b_pd, b_pd, 26, at_x(xl)),
        mcopy(lo_pd, lo_pd, 27, other),
        mcopy(ro_pd, ro_pd, 28, other),
    ]
    pd_last = mcopy(oo_pd, oo_pd, 29, other)

    def final_core(k):
        return [mcopy(fs.at[1 - c, k], fr.at[k], 9 + k, other)]

    def final_half(k):
        return [
            mcopy(fs.at[c, k, xo, 0:32], th.at[0, k], 17 + k, at_x(xr)),
            mcopy(fs.at[c, k, xo, 32:64], th.at[1, k], 19 + k, at_x(xl)),
        ]

    def final_full(k):
        return [
            mcopy(fs.at[c, k, xr], tf.at[0, k], 12 + k, at_x(xr)),
            mcopy(fs.at[c, k, xl], tf.at[1, k], 14 + k, at_x(xl)),
        ]

    def reach_core(k, acc):
        for b in range(8):
            fs[b % 2, k, b // 2] = acc[b * 64 : b * 64 + 64].astype(BF16)
        start(final_core(k))

    def reach_half(k):
        wait(final_core(k))
        add_into(fs.at[c, k], fr.at[k])
        start(final_half(k))

    def reach_full(k):
        wait(final_half(k))
        add_into(fs.at[c, k, xr, 0:32], th.at[0, k])
        add_into(fs.at[c, k, xl, 32:64], th.at[1, k])
        start(final_full(k))

    def final_sum(k):
        wait(final_full(k))
        return fs[c, k, x].astype(F32) + tf[0, k].astype(F32) + tf[1, k].astype(F32)

    @pl.loop(0, GROUPS + STAGES - 1)
    def _(t):
        for s in range(STAGES + 1):
            j = t - s if s < STAGES else t - s + 1
            if s == 4:

                @pl.when(t == 4)
                def _():
                    spread_wait(nbz, 2)
                    n = jnp.sqrt(sum(nbz[k].astype(F32) for k in range(4)) + EPS)
                    nrm[...] = n
                    for k, mag in enumerate((gmag, umag)):
                        for g in range(GROUPS):
                            scl[k * 8 + g : k * 8 + g + 1] = mag[g * 512 : g * 512 + 512].reshape(1, 512)
                    scl[...] = scl[...] / n

            if s == STAGES - 1:

                @pl.when(t == STAGES - 1)
                def _():
                    wait([pd_core, pd_last])
                    pr[...] = jnp.transpose(pd[...].reshape(512, 128).astype(F32))[0:48].astype(BF16)

            if s == STAGES:

                @pl.when(t == GROUPS + STAGES - 2)
                def _():
                    reach_core(0, oacc)

            @pl.when(jnp.logical_and(j >= 0, j < GROUPS))
            def _():
                @pl.loop(0, 2)
                def _(h):
                    stage(s, j, h)

        @pl.when(t == 0)
        def _():
            lpad[...] = jnp.zeros_like(lpad)
            dpad[...] = jnp.zeros_like(dpad)
            lpad[0:16] = glt[...]
            lpad[16:32] = ult[...]
            dpad[32:48] = dr[...]
            own_z = (cot[...].astype(F32) * scd[1:2]).astype(BF16)
            pry[y] = (nt(tok[...], lpad[...]) + nt(own_z, dpad[...])).astype(BF16)
            ring_own(pry, y, at_y, 3)

        @pl.when(t < 2)
        def _():
            @pl.loop(2 * t + 1, 4 * t + 3)
            def _(g):
                merge_gu(g)

        @pl.when(t == 1)
        def _():
            nby[y] = nf[...].astype(BF16)
            ring_own(nby, y, at_y, 14)
            ring_pass(pry, y, at_y, 3)

        @pl.when(t == 2)
        def _():
            ring_pass(nby, y, at_y, 14)
            ring_wait(pry, 3)
            prz[z] = sum(pry[k].astype(F32) for k in range(4)).astype(BF16)
            ring_own(prz, z, at_z, 5)

        @pl.when(t == 3)
        def _():
            oacc[...] = jnp.zeros_like(oacc)
            xacc[...] = jnp.zeros_like(xacc)
            bk[...] = jnp.zeros_like(bk)
            ring_pass(prz, z, at_z, 5)
            ring_wait(nby, 14)
            nbz[z] = sum(nby[k].astype(F32) for k in range(4)).astype(BF16)
            spread(nbz, z, at_z, 2)

        @pl.when(t == 4)
        def _():
            ring_wait(prz, 5)
            pd[x, c] = sum(prz[k].astype(F32) for k in range(4)).astype(BF16)
            pd_core.start()
            pd_right.start()
            pd_left.start()

        @pl.when(t == 5)
        def _():
            wait([pd_right, pd_left])
            start(pd_pass)

        @pl.when(t == 6)
        def _():
            wait(pd_pass)
            pd_last.start()

        @pl.when(t == GROUPS + 3)
        def _():
            mgy[y] = mf[...].astype(BF16)
            ring_own(mgy, y, at_y, 7)

        @pl.when(t == GROUPS + 4)
        def _():
            ring_pass(mgy, y, at_y, 7)

        @pl.when(t == GROUPS + 5)
        def _():
            ring_wait(mgy, 7)
            mgz[z] = sum(mgy[k].astype(F32) for k in range(4)).astype(BF16)
            ring_own(mgz, z, at_z, 9)

        @pl.when(t == GROUPS + 6)
        def _():
            ring_pass(mgz, z, at_z, 9)

    smd[dp] = bk[:, pl.ds(pl.multiple_of(y * 128, 128), 128)].astype(BF16)
    for d in range(1, 8):
        rcopy(smd.at[dp], smd.at[dp], spread_s.at[11], spread_r.at[11], ((dp + d) % 8, mp)).start()
    reach_core(1, xacc)
    md_core = mcopy(mdc.at[c], mdc.at[c], 11, other)
    reach_half(0)
    mdc[c] = jnp.sum(oacc[...] * gath[1].reshape(512, 512).astype(F32), axis=0, keepdims=True)
    md_core.start()
    reach_half(1)
    landed(smd.at[0:7], spread_s.at[11])
    landed(smd.at[0:7], spread_r.at[11])
    smy[y] = sum(smd[k].astype(F32) for k in range(8)).astype(BF16)
    spread(smy, y, at_y, 12)
    reach_full(0)
    md_core.wait()
    mdx[x] = mdc[0] + mdc[1]
    spread(mdx, x, at_x, 13)
    reach_full(1)

    ring_wait(mgz, 9)
    mags = sum(mgz[k].astype(F32) for k in range(4)) / nrm[...]
    for g in range(GROUPS):
        ggm[:, g * 512 : g * 512 + 512] = mags[g : g + 1]
        gum[:, g * 512 : g * 512 + 512] = mags[8 + g : 9 + g]
    spread_wait(smy, 12)
    for k in range(4):
        back[:, k * 128 : k * 128 + 128] = smy[k]
    lg = nn(back[0:32], tokens())
    ggl[...] = lg[0:16]
    gul[...] = lg[16:32]
    gdr[...] = nn(back[32:48], zt[...])
    spread_wait(mdx, 13)
    gdm[...] = (mdx[0] + mdx[1] + mdx[2] + mdx[3]) / scd[0:1]
    out[...] = (final_sum(0) * scd[1:2]).astype(BF16)
    dx[...] = final_sum(1).astype(BF16)


def per_device(tok, fg, fu, fd, gl, gr, ul, ur, dl, dr, gmag, umag, dmag, cot):
    vm = pl.BlockSpec(memory_space=pltpu.VMEM)
    hbm = pl.BlockSpec(memory_space=pl.ANY)
    f = jax.ShapeDtypeStruct
    V = pltpu.VMEM
    G, C = GROUPS, HALF
    call = pl.pallas_call(
        kernel,
        out_shape=(
            f((64, 512), BF16), f((64, 512), BF16),
            f((1, 3584), F32), f((1, 3584), F32), f((1, 512), F32),
            f((16, 3584), F32), f((16, 512), F32), f((16, 3584), F32), f((16, 512), F32),
            f((16, 512), F32), f((16, 3584), F32),
        ),
        in_specs=[vm, vm, hbm, hbm, hbm] + [vm] * 9,
        out_specs=(vm,) * 11,
        scratch_shapes=[
            V((G, 2, 512, C), BF16), V((G, 2, 512, C), BF16), V((G, 2, C, 512), BF16),
            V((2, 4, 2, 64, 512), BF16), V((512, 512), BF16),
            V((2, 1, 512), F32), V((4, 1, 512), F32), V((2, 512), F32),
            V((16, 512), F32), V((4, 16, 512), BF16), V((4, 16, 512), BF16), V((16, 512), F32), V((16, 512), F32),
            V((128, 512), BF16), V((128, 512), BF16),
            V((4, 64, 128), BF16), V((4, 64, 128), BF16), V((4, 2, 64, 128), BF16), V((48, 512), BF16),
            V((G, 2, 3, 4, 4, 32, C), BF16),
            V((G, 2, 2, 3, 2, 32, C), BF16), V((G, 2, 2, 3, 4, 32, C), BF16),
            V((G, 2, 3, 4, 32, C), BF16),
            V((G, 2, 2, 3, 16, C), BF16), V((G, 2, 2, 3, 32, C), BF16),
            V((G, 2, 3, 4, 4, 32, C), BF16),
            V((16, 512), F32), V((4, 16, 512), BF16), V((4, 16, 512), BF16),
            V((512, 512), F32), V((512, 512), F32), V((48, 512), F32),
            V((2, 2, 4, 64, 512), BF16), V((2, 4, 64, 512), BF16),
            V((2, 2, 32, 512), BF16), V((2, 2, 64, 512), BF16),
            V((8, 48, 128), BF16), V((4, 48, 128), BF16), V((48, 512), BF16),
            V((2, 1, 512), F32), V((4, 1, 512), F32),
            pltpu.SemaphoreType.DMA((3, G)),
            pltpu.SemaphoreType.DMA((8, 2, 2)),
            pltpu.SemaphoreType.DMA((8, 3, 2)),
            pltpu.SemaphoreType.DMA((30,)),
            pltpu.SemaphoreType.DMA((30,)),
            pltpu.SemaphoreType.DMA((16,)),
            pltpu.SemaphoreType.DMA((16,)),
        ],
        compiler_params=pltpu.CompilerParams(
            collective_id=0, has_side_effects=True, vmem_limit_bytes=63 * 1024 * 1024
        ),
    )
    res = call(tok, cot, fg, fu, fd, gl.T, gr, ul.T, ur, dl.T, dr, gmag, umag, dmag)
    flat = (2, 3, 4)

    def finish(*refs):
        for k in range(11):
            value = refs[k][...]
            refs[k + 11][...] = value.reshape(-1) if k in flat else value

    o, d, ggm, gum, gdm, ggr, ggl, gur, gul, gdr, gdl = pl.pallas_call(
        finish,
        out_shape=tuple(
            f((r.size,) if k in flat else r.shape, r.dtype) for k, r in enumerate(res)
        ),
        in_specs=[vm] * 11,
        out_specs=(vm,) * 11,
    )(*res)
    return o, d, ggm, gum, gdm, ggr, ggl.T, gur, gul.T, gdr, gdl.T


def solution(mesh):
    in_specs = (
        P("dp", "mp"), P("mp", "dp"), P("mp", "dp"), P("dp", "mp"),
        P("mp", None), P(None, "dp"), P("mp", None), P(None, "dp"),
        P("dp", None), P(None, "mp"), P("dp"), P("dp"), P("mp"), P("dp", "mp"),
    )
    out_specs = (
        P("dp", "mp"), P("dp", "mp"), P("dp"), P("dp"), P("mp"),
        P(None, "dp"), P("mp", None), P(None, "dp"), P("mp", None), P(None, "mp"), P("dp", None),
    )
    return jax.shard_map(
        per_device, mesh=mesh, in_specs=in_specs, out_specs=out_specs, check_vma=False
    )
```

```python
import jax
import jax.numpy as jnp
from jax import lax
from jax.experimental import pallas as pl
from jax.experimental.pallas import tpu as pltpu
from jax.sharding import PartitionSpec as P

F32 = jnp.float32
BF16 = jnp.bfloat16
MESH = pl.DeviceIdType.MESH
EPS = 1e-06

GROUPS = 7
HALF = 256
STAGES = 9


def nn(a, b):
    return jnp.dot(a, b, preferred_element_type=F32)


def nt(a, b):
    return lax.dot_general(a, b, (((1,), (1,)), ((), ())), preferred_element_type=F32)


def tn(a, b):
    return lax.dot_general(a, b, (((0,), (0,)), ((), ())), preferred_element_type=F32)


def kernel(
    tok, cot, wg_hbm, wu_hbm, wd_hbm, glt, gr, ult, ur, dlt, dr, gmag, umag, dmag,
    out, dx, ggm, gum, gdm, ggr, ggl, gur, gul, gdr, gdl,
    wg, wu, wd, gath, zt, sqd_c, sqd_x, scd, nf, nby, nbz, scl, nrm, lpad, dpad, pry, prz, pd, pr,
    part, r1h, r1f, q, r2h, r2f, hz, mf, mgy, mgz, oacc, xacc, bk,
    fs, fr, th, tf, smd, smy, back, mdc, mdx,
    wsem, ssem, rsem, ms, mr, spread_s, spread_r,
):
    dp = lax.axis_index("dp")
    mp = lax.axis_index("mp")
    x, c = dp // 2, dp % 2
    y, z = mp // 4, mp % 4

    def at_x(i):
        return (i * 2 + c, mp)

    def at_y(i):
        return (dp, i * 4 + z)

    def at_z(i):
        return (dp, y * 4 + i)

    def at_x_other(i):
        return (i * 2 + 1 - c, mp)

    other = at_x_other(x)

    def rcopy(src, dst, s, r, dev):
        return pltpu.make_async_remote_copy(
            src_ref=src, dst_ref=dst, send_sem=s, recv_sem=r, device_id=dev, device_id_type=MESH
        )

    def mcopy(src, dst, k, dev):
        return rcopy(src, dst, ms.at[k], mr.at[k], dev)

    def landed(ref, sem):
        pltpu.make_async_copy(ref, ref, sem).wait()

    def spread(slots, me, place, k):
        for d in (1, 2, 3):
            rcopy(
                slots.at[me], slots.at[me], spread_s.at[k], spread_r.at[k], place((me + d) % 4)
            ).start()

    def spread_wait(slots, k):
        landed(slots.at[0:3], spread_s.at[k])
        landed(slots.at[0:3], spread_r.at[k])

    def ring_own(slots, me, place, k):
        for i in ((me + 1) % 4, (me + 3) % 4):
            rcopy(slots.at[me], slots.at[me], spread_s.at[k], spread_r.at[k], place(i)).start()

    def ring_pass(slots, me, place, k):
        landed(slots.at[0:2], spread_s.at[k])
        landed(slots.at[0:2], spread_r.at[k])
        axis = 2 if slots.shape[2] > 128 else 1
        half = slots.shape[axis] // 2
        right, left = (me + 1) % 4, (me + 3) % 4
        if axis == 2:
            a, b = slots.at[left, :, 0:half], slots.at[right, :, half:]
        else:
            a, b = slots.at[left, 0:half], slots.at[right, half:]
        rcopy(a, a, spread_s.at[k + 1], spread_r.at[k + 1], place(right)).start()
        rcopy(b, b, spread_s.at[k + 1], spread_r.at[k + 1], place(left)).start()

    def ring_wait(slots, k):
        landed(slots.at[0], spread_s.at[k + 1])
        landed(slots.at[0], spread_r.at[k + 1])

    def start(copies):
        for cp in copies:
            cp.start()

    def wait(copies):
        for cp in copies:
            cp.wait()

    def load_d(j, h):
        return pltpu.make_async_copy(
            wd_hbm.at[pl.ds(pl.multiple_of((j * 2 + h) * HALF, HALF), HALF)],
            wd.at[j, h],
            wsem.at[0, j],
        )

    def load_gu(w_hbm, w, k, j, h):
        return pltpu.make_async_copy(
            w_hbm.at[:, pl.ds(pl.multiple_of((j * 2 + h) * HALF, HALF), HALF)],
            w.at[j, h],
            wsem.at[k, j],
        )

    @pl.loop(0, GROUPS)
    def _(j):
        for h in (0, 1):
            load_d(j, h).start()

    @pl.loop(0, GROUPS)
    def _(j):
        for h in (0, 1):
            load_gu(wg_hbm, wg, 1, j, h).start()
            load_gu(wu_hbm, wu, 2, j, h).start()

    gath[0, x, c] = tok[...]
    gath[1, x, c] = cot[...]

    barrier = pltpu.get_barrier_semaphore()
    for d in (1, 2, 3):
        for dev in (at_x((x + d) % 4), at_y((y + d) % 4), at_z((z + d) % 4)):
            pl.semaphore_signal(barrier, inc=1, device_id=dev, device_id_type=MESH)
    for dev in (other, *(at_x_other((x + d) % 4) for d in (1, 2, 3))):
        pl.semaphore_signal(barrier, inc=1, device_id=dev, device_id_type=MESH)
    pl.semaphore_wait(barrier, 13)

    xr, xl, xo = (x + 1) % 4, (x + 3) % 4, (x + 2) % 4
    own = gath.at[:, x, c]
    g_own = [
        mcopy(own, own, 0, at_x(xr)),
        mcopy(own, own, 1, at_x(xl)),
        mcopy(own, own, 2, other),
    ]
    start(g_own)

    def merge_down(j, total):
        landed(wd.at[j], wsem.at[0, j])
        for h in (0, 1):
            rows = pl.ds(pl.multiple_of((j * 2 + h) * HALF, HALF), HALF)
            m = wd[j, h].astype(F32) + tn(dlt[:, rows], dr[...])
            wd[j, h] = m.astype(BF16)
            total = total + jnp.sum(m * m, axis=0, keepdims=True)
        return total

    sqd_c[c] = lax.fori_loop(0, GROUPS, merge_down, jnp.zeros((1, 512), F32))
    s_core = mcopy(sqd_c.at[c], sqd_c.at[c], 3, other)
    s_core.start()

    wait(g_own[:2])
    lo, ro = gath.at[:, xl, c], gath.at[:, xr, c]
    a, b = gath.at[:, xl, c, 0:32], gath.at[:, xr, c, 32:64]
    g_fwd = [
        mcopy(a, a, 4, at_x(xr)),
        mcopy(b, b, 5, at_x(xl)),
        mcopy(a, a, 6, at_x_other(xr)),
        mcopy(b, b, 7, at_x_other(xl)),
        mcopy(lo, lo, 8, other),
        mcopy(ro, ro, 16, other),
    ]
    start(g_fwd)

    def merge_gu(j):
        for k, w, left, right in ((0, wg, glt, gr), (1, wu, ult, ur)):
            landed(w.at[j], wsem.at[k + 1, j])
            for h in (0, 1):
                cols = pl.ds(pl.multiple_of((j * 2 + h) * HALF, HALF), HALF)
                m = w[j, h].astype(F32) + tn(left[...], right[:, cols])
                w[j, h] = m.astype(BF16)
                nf[pl.ds(k * 8 + j, 1), h * HALF : (h + 1) * HALF] = jnp.sum(m * m, axis=0, keepdims=True)

    s_core.wait()
    sqd_x[x] = sqd_c[0] + sqd_c[1]
    spread(sqd_x, x, at_x, 0)
    merge_gu(0)
    merge_gu(1)

    spread_wait(sqd_x, 0)
    sqd = sqd_x[0] + sqd_x[1] + sqd_x[2] + sqd_x[3]
    normd = jnp.sqrt(sqd + EPS)
    scd[0:1] = normd
    scd[1:2] = dmag[...].reshape(1, 512) / normd
    g_own[2].wait()
    wait(g_fwd)

    nf[7:8] = jnp.ones((1, 512), F32)
    nf[15:16] = jnp.ones((1, 512), F32)
    scl[...] = jnp.ones_like(scl)
    mf[...] = jnp.zeros_like(mf)

    def tokens():
        return gath[0].reshape(512, 512)

    zt[...] = (gath[1].reshape(512, 512).astype(F32) * scd[1:2]).astype(BF16)

    def geometry(h):
        ia = y + h * (z - y)
        ib = z + h * (y - z)

        def at_a(i):
            return (dp, (i + h * (y - i)) * 4 + z + h * (i - z))

        def at_b(i):
            return (dp, (y + h * (i - y)) * 4 + i + h * (z - i))

        return ia, ib, at_a, at_b

    def copies(s, j, h):
        ia, ib, at_a, at_b = geometry(h)
        ar, al, ao = (ia + 1) % 4, (ia + 3) % 4, (ia + 2) % 4
        br, bl, bo = (ib + 1) % 4, (ib + 3) % 4, (ib + 2) % 4
        if s == 0:
            a = part.at[j, h, :, ao, 0:2], r1h.at[j, h, 0]
            b = part.at[j, h, :, ao, 2:4], r1h.at[j, h, 1]
        elif s == 1:
            a = part.at[j, h, :, ar], r1f.at[j, h, 0]
            b = part.at[j, h, :, al], r1f.at[j, h, 1]
        elif s == 2:
            a = q.at[j, h, :, bo, 0:16], r2h.at[j, h, 0]
            b = q.at[j, h, :, bo, 16:32], r2h.at[j, h, 1]
        elif s == 3:
            a = q.at[j, h, :, br], r2f.at[j, h, 0]
            b = q.at[j, h, :, bl], r2f.at[j, h, 1]
        elif s == 4:
            a = b = (hz.at[j, h, :, ia, ib],) * 2
        elif s == 5:
            a = (hz.at[j, h, :, ia, bl, 0:16],) * 2
            b = (hz.at[j, h, :, ia, br, 16:32],) * 2
        elif s == 6:
            a = b = (hz.at[j, h, :, ia],) * 2
        else:
            a = (hz.at[j, h, :, al, 0:2],) * 2
            b = (hz.at[j, h, :, ar, 2:4],) * 2
        if s in (0, 1, 6, 7):
            dr_, dl_ = at_a(ar), at_a(al)
        else:
            dr_, dl_ = at_b(br), at_b(bl)
        return [
            rcopy(*a, ssem.at[s, j % 2, h], rsem.at[s, j % 4, h], dr_),
            rcopy(*b, ssem.at[s, j % 2, h], rsem.at[s, j % 4, h], dl_),
        ]

    def arrived(s, j, h):
        both = (
            r1h.at[j, h], r1f.at[j, h], r2h.at[j, h], r2f.at[j, h],
            hz.at[j, h, :, 0, 0:2], hz.at[j, h, :, 0, 0], hz.at[j, h, :, 0:2], hz.at[j, h, :, 0],
        )[s]
        landed(both, ssem.at[s, j % 2, h])
        landed(both, rsem.at[s, j % 4, h])

    def add_into(ref, extra):
        ref[...] = (ref[...].astype(F32) + extra[...].astype(F32)).astype(BF16)

    def stage(s, j, h):
        ia, ib, _, _ = geometry(h)
        ar, al = (ia + 1) % 4, (ia + 3) % 4
        br, bl = (ib + 1) % 4, (ib + 3) % 4
        cols = pl.ds(pl.multiple_of((j * 2 + h) * HALF, HALF), HALF)
        if 0 < s < 9:
            arrived(s - 1, j, h)
        if s == 0:
            part[j, h, 0] = nn(tokens(), wg[j, h]).astype(BF16).reshape(4, 4, 32, HALF)
            part[j, h, 1] = nn(tokens(), wu[j, h]).astype(BF16).reshape(4, 4, 32, HALF)
            part[j, h, 2] = nt(zt[...], wd[j, h]).astype(BF16).reshape(4, 4, 32, HALF)
        elif s == 1:
            add_into(part.at[j, h, :, ar, 0:2], r1h.at[j, h, 0])
            add_into(part.at[j, h, :, al, 2:4], r1h.at[j, h, 1])
        elif s == 2:
            q[j, h] = (
                part[j, h, :, ia].astype(F32)
                + r1f[j, h, 0].astype(F32)
                + r1f[j, h, 1].astype(F32)
            ).astype(BF16)
        elif s == 3:
            add_into(q.at[j, h, :, br, 0:16], r2h.at[j, h, 0])
            add_into(q.at[j, h, :, bl, 16:32], r2h.at[j, h, 1])
        elif s == 4:
            pg, pu, gh = (
                q[j, h, k, ib].astype(F32) + r2f[j, h, 0, k].astype(F32) + r2f[j, h, 1, k].astype(F32)
                for k in range(3)
            )
            local = pl.ds(pl.multiple_of(h * HALF, HALF), HALF)
            sg, su = scl[pl.ds(j, 1), local], scl[pl.ds(8 + j, 1), local]
            ga, ua = pg * sg, pu * su
            sig = 1.0 / (1.0 + jnp.exp(-ga))
            silu = ga * sig
            dg = gh * ua * sig * (1.0 + ga * (1.0 - sig))
            du = gh * silu
            hz[j, h, 0, ia, ib] = (silu * ua).astype(BF16)
            hz[j, h, 1, ia, ib] = (dg * sg).astype(BF16)
            hz[j, h, 2, ia, ib] = (du * su).astype(BF16)
            mf[pl.ds(j, 1), local] = jnp.sum(dg * pg, axis=0, keepdims=True)
            mf[pl.ds(8 + j, 1), local] = jnp.sum(du * pu, axis=0, keepdims=True)
        elif s == 8:
            hid = hz[j, h, 0].reshape(512, HALF)
            oacc[...] += nn(hid, wd[j, h])
            gdl[:, cols] = nn(pr[32:48], hid)
            bk[32:48] += nt(dlt[:, cols], hid)
        elif s == 9:
            zg = hz[j, h, 1].reshape(512, HALF)
            zu = hz[j, h, 2].reshape(512, HALF)
            xacc[...] += nt(zg, wg[j, h]) + nt(zu, wu[j, h])
            ggr[:, cols] = nn(pr[0:16], zg)
            gur[:, cols] = nn(pr[16:32], zu)
            bk[0:16] += nt(gr[:, cols], zg)
            bk[16:32] += nt(ur[:, cols], zu)
        if s < 8:
            start(copies(s, j, h))

    own_pd = pd.at[x, c]
    pd_core = mcopy(own_pd, own_pd, 22, other)
    pd_right = mcopy(own_pd, own_pd, 23, at_x(xr))
    pd_left = mcopy(own_pd, own_pd, 24, at_x(xl))
    lo_pd, ro_pd, oo_pd = pd.at[xl, c], pd.at[xr, c], pd.at[xo, c]
    a_pd, b_pd = pd.at[xl, c, 0:32], pd.at[xr, c, 32:64]
    pd_pass = [
        mcopy(a_pd, a_pd, 25, at_x(xr)),
        mcopy(b_pd, b_pd, 26, at_x(xl)),
        mcopy(lo_pd, lo_pd, 27, other),
        mcopy(ro_pd, ro_pd, 28, other),
    ]
    pd_last = mcopy(oo_pd, oo_pd, 29, other)

    def final_core(k):
        return [mcopy(fs.at[1 - c, k], fr.at[k], 9 + k, other)]

    def final_half(k):
        return [
            mcopy(fs.at[c, k, xo, 0:32], th.at[0, k], 17 + k, at_x(xr)),
            mcopy(fs.at[c, k, xo, 32:64], th.at[1, k], 19 + k, at_x(xl)),
        ]

    def final_full(k):
        return [
            mcopy(fs.at[c, k, xr], tf.at[0, k], 12 + k, at_x(xr)),
            mcopy(fs.at[c, k, xl], tf.at[1, k], 14 + k, at_x(xl)),
        ]

    def reach_core(k, acc):
        for b in range(8):
            fs[b % 2, k, b // 2] = acc[b * 64 : b * 64 + 64].astype(BF16)
        start(final_core(k))

    def reach_half(k):
        wait(final_core(k))
        add_into(fs.at[c, k], fr.at[k])
        start(final_half(k))

    def reach_full(k):
        wait(final_half(k))
        add_into(fs.at[c, k, xr, 0:32], th.at[0, k])
        add_into(fs.at[c, k, xl, 32:64], th.at[1, k])
        start(final_full(k))

    def final_sum(k):
        wait(final_full(k))
        return fs[c, k, x].astype(F32) + tf[0, k].astype(F32) + tf[1, k].astype(F32)

    @pl.loop(0, 2)
    def _(h):
        stage(0, 0, h)

    @pl.loop(0, GROUPS + STAGES - 1)
    def _(t):
        for s in range(STAGES + 1):
            j = t + 1 if s == 0 else t - s if s < STAGES else t - s + 1
            if s == 4:

                @pl.when(t == 4)
                def _():
                    spread_wait(nbz, 2)
                    n = jnp.sqrt(sum(nbz[k].astype(F32) for k in range(4)) + EPS)
                    nrm[...] = n
                    for k, mag in enumerate((gmag, umag)):
                        for g in range(GROUPS):
                            scl[k * 8 + g : k * 8 + g + 1] = mag[g * 512 : g * 512 + 512].reshape(1, 512)
                    scl[...] = scl[...] / n

            if s == STAGES - 1:

                @pl.when(t == STAGES - 1)
                def _():
                    wait([pd_core, pd_last])
                    pr[...] = jnp.transpose(pd[...].reshape(512, 128).astype(F32))[0:48].astype(BF16)

            if s == STAGES:

                @pl.when(t == GROUPS + STAGES - 2)
                def _():
                    reach_core(0, oacc)

            @pl.when(jnp.logical_and(j >= 0, j < GROUPS))
            def _():
                @pl.loop(0, 2)
                def _(h):
                    stage(s, j, h)

        @pl.when(t == 0)
        def _():
            lpad[...] = jnp.zeros_like(lpad)
            dpad[...] = jnp.zeros_like(dpad)
            lpad[0:16] = glt[...]
            lpad[16:32] = ult[...]
            dpad[32:48] = dr[...]
            own_z = (cot[...].astype(F32) * scd[1:2]).astype(BF16)
            pry[y] = (nt(tok[...], lpad[...]) + nt(own_z, dpad[...])).astype(BF16)
            ring_own(pry, y, at_y, 3)

        @pl.when(t < 2)
        def _():
            @pl.loop(2 * t + 2, 3 * t + 4)
            def _(g):
                merge_gu(g)

        @pl.when(t == 1)
        def _():
            nby[y] = nf[...].astype(BF16)
            ring_own(nby, y, at_y, 14)
            ring_pass(pry, y, at_y, 3)

        @pl.when(t == 2)
        def _():
            ring_pass(nby, y, at_y, 14)
            ring_wait(pry, 3)
            prz[z] = sum(pry[k].astype(F32) for k in range(4)).astype(BF16)
            ring_own(prz, z, at_z, 5)

        @pl.when(t == 3)
        def _():
            oacc[...] = jnp.zeros_like(oacc)
            xacc[...] = jnp.zeros_like(xacc)
            bk[...] = jnp.zeros_like(bk)
            ring_pass(prz, z, at_z, 5)
            ring_wait(nby, 14)
            nbz[z] = sum(nby[k].astype(F32) for k in range(4)).astype(BF16)
            spread(nbz, z, at_z, 2)

        @pl.when(t == 4)
        def _():
            ring_wait(prz, 5)
            pd[x, c] = sum(prz[k].astype(F32) for k in range(4)).astype(BF16)
            pd_core.start()
            pd_right.start()
            pd_left.start()

        @pl.when(t == 5)
        def _():
            wait([pd_right, pd_left])
            start(pd_pass)

        @pl.when(t == 6)
        def _():
            wait(pd_pass)
            pd_last.start()

        @pl.when(t == GROUPS + 3)
        def _():
            mgy[y] = mf[...].astype(BF16)
            ring_own(mgy, y, at_y, 7)

        @pl.when(t == GROUPS + 4)
        def _():
            ring_pass(mgy, y, at_y, 7)

        @pl.when(t == GROUPS + 5)
        def _():
            ring_wait(mgy, 7)
            mgz[z] = sum(mgy[k].astype(F32) for k in range(4)).astype(BF16)
            ring_own(mgz, z, at_z, 9)

        @pl.when(t == GROUPS + 6)
        def _():
            ring_pass(mgz, z, at_z, 9)

    smd[dp] = bk[:, pl.ds(pl.multiple_of(y * 128, 128), 128)].astype(BF16)
    for d in range(1, 8):
        rcopy(smd.at[dp], smd.at[dp], spread_s.at[11], spread_r.at[11], ((dp + d) % 8, mp)).start()
    reach_core(1, xacc)
    md_core = mcopy(mdc.at[c], mdc.at[c], 11, other)
    reach_half(0)
    mdc[c] = jnp.sum(oacc[...] * gath[1].reshape(512, 512).astype(F32), axis=0, keepdims=True)
    md_core.start()
    reach_half(1)
    landed(smd.at[0:7], spread_s.at[11])
    landed(smd.at[0:7], spread_r.at[11])
    smy[y] = sum(smd[k].astype(F32) for k in range(8)).astype(BF16)
    spread(smy, y, at_y, 12)
    reach_full(0)
    md_core.wait()
    mdx[x] = mdc[0] + mdc[1]
    spread(mdx, x, at_x, 13)
    reach_full(1)

    ring_wait(mgz, 9)
    mags = sum(mgz[k].astype(F32) for k in range(4)) / nrm[...]
    for g in range(GROUPS):
        ggm[:, g * 512 : g * 512 + 512] = mags[g : g + 1]
        gum[:, g * 512 : g * 512 + 512] = mags[8 + g : 9 + g]
    spread_wait(smy, 12)
    for k in range(4):
        back[:, k * 128 : k * 128 + 128] = smy[k]
    lg = nn(back[0:32], tokens())
    ggl[...] = lg[0:16]
    gul[...] = lg[16:32]
    gdr[...] = nn(back[32:48], zt[...])
    spread_wait(mdx, 13)
    gdm[...] = (mdx[0] + mdx[1] + mdx[2] + mdx[3]) / scd[0:1]
    out[...] = (final_sum(0) * scd[1:2]).astype(BF16)
    dx[...] = final_sum(1).astype(BF16)


def per_device(tok, fg, fu, fd, gl, gr, ul, ur, dl, dr, gmag, umag, dmag, cot):
    vm = pl.BlockSpec(memory_space=pltpu.VMEM)
    hbm = pl.BlockSpec(memory_space=pl.ANY)
    f = jax.ShapeDtypeStruct
    V = pltpu.VMEM
    G, C = GROUPS, HALF
    call = pl.pallas_call(
        kernel,
        out_shape=(
            f((64, 512), BF16), f((64, 512), BF16),
            f((1, 3584), F32), f((1, 3584), F32), f((1, 512), F32),
            f((16, 3584), F32), f((16, 512), F32), f((16, 3584), F32), f((16, 512), F32),
            f((16, 512), F32), f((16, 3584), F32),
        ),
        in_specs=[vm, vm, hbm, hbm, hbm] + [vm] * 9,
        out_specs=(vm,) * 11,
        scratch_shapes=[
            V((G, 2, 512, C), BF16), V((G, 2, 512, C), BF16), V((G, 2, C, 512), BF16),
            V((2, 4, 2, 64, 512), BF16), V((512, 512), BF16),
            V((2, 1, 512), F32), V((4, 1, 512), F32), V((2, 512), F32),
            V((16, 512), F32), V((4, 16, 512), BF16), V((4, 16, 512), BF16), V((16, 512), F32), V((16, 512), F32),
            V((128, 512), BF16), V((128, 512), BF16),
            V((4, 64, 128), BF16), V((4, 64, 128), BF16), V((4, 2, 64, 128), BF16), V((48, 512), BF16),
            V((G, 2, 3, 4, 4, 32, C), BF16),
            V((G, 2, 2, 3, 2, 32, C), BF16), V((G, 2, 2, 3, 4, 32, C), BF16),
            V((G, 2, 3, 4, 32, C), BF16),
            V((G, 2, 2, 3, 16, C), BF16), V((G, 2, 2, 3, 32, C), BF16),
            V((G, 2, 3, 4, 4, 32, C), BF16),
            V((16, 512), F32), V((4, 16, 512), BF16), V((4, 16, 512), BF16),
            V((512, 512), F32), V((512, 512), F32), V((48, 512), F32),
            V((2, 2, 4, 64, 512), BF16), V((2, 4, 64, 512), BF16),
            V((2, 2, 32, 512), BF16), V((2, 2, 64, 512), BF16),
            V((8, 48, 128), BF16), V((4, 48, 128), BF16), V((48, 512), BF16),
            V((2, 1, 512), F32), V((4, 1, 512), F32),
            pltpu.SemaphoreType.DMA((3, G)),
            pltpu.SemaphoreType.DMA((8, 2, 2)),
            pltpu.SemaphoreType.DMA((8, 4, 2)),
            pltpu.SemaphoreType.DMA((30,)),
            pltpu.SemaphoreType.DMA((30,)),
            pltpu.SemaphoreType.DMA((16,)),
            pltpu.SemaphoreType.DMA((16,)),
        ],
        compiler_params=pltpu.CompilerParams(
            collective_id=0, has_side_effects=True, vmem_limit_bytes=63 * 1024 * 1024
        ),
    )
    res = call(tok, cot, fg, fu, fd, gl.T, gr, ul.T, ur, dl.T, dr, gmag, umag, dmag)
    flat = (2, 3, 4)

    def finish(*refs):
        for k in range(11):
            value = refs[k][...]
            refs[k + 11][...] = value.reshape(-1) if k in flat else value

    o, d, ggm, gum, gdm, ggr, ggl, gur, gul, gdr, gdl = pl.pallas_call(
        finish,
        out_shape=tuple(
            f((r.size,) if k in flat else r.shape, r.dtype) for k, r in enumerate(res)
        ),
        in_specs=[vm] * 11,
        out_specs=(vm,) * 11,
    )(*res)
    return o, d, ggm, gum, gdm, ggr, ggl.T, gur, gul.T, gdr, gdl.T


def solution(mesh):
    in_specs = (
        P("dp", "mp"), P("mp", "dp"), P("mp", "dp"), P("dp", "mp"),
        P("mp", None), P(None, "dp"), P("mp", None), P(None, "dp"),
        P("dp", None), P(None, "mp"), P("dp"), P("dp"), P("mp"), P("dp", "mp"),
    )
    out_specs = (
        P("dp", "mp"), P("dp", "mp"), P("dp"), P("dp"), P("mp"),
        P(None, "dp"), P("mp", None), P(None, "dp"), P("mp", None), P(None, "mp"), P("dp", None),
    )
    return jax.shard_map(
        per_device, mesh=mesh, in_specs=in_specs, out_specs=out_specs, check_vma=False
    )
```
